512 devices in a mesh: grp: 16 (over y_lo, x), chan: 32 (over y_hi, z, core).
Axes of the slice: x: 4, y: 8 (y_hi: 2, y_lo: 4; y = y_hi * 4 + y_lo), z: 8, core: 2. Of those that a mesh axis runs over, the one named last changes fastest.
Arguments:
- voltages: bfloat16 [512, 2, 2, 77824], P(('grp', 'chan')), may hold values from -6 to 6
- beam_weights: bfloat16 [512, 4096, 2, 128], P('grp', 'chan'), may hold values from -0.25 to 0.25
- owner_table: int32 [4096], replicated, may hold values from 0 to 4095, each once
- live_stations: int32 [512], P(('grp', 'chan')), may hold values 0 or 1
Outputs:
- beams: float32 [128, 2, 2, 4, 4096], P('grp', None, None, None, 'chan')
The draws below stay inside these ranges and needn't reach their ends.
Inputs may be any that keep to these rules, and one draw needn't show every extreme that they name: `owner_table`: each of the 4096 channels appears exactly once.
All inputs are finite; a program needn't handle non-finite values. No bound on the sum of `live_stations` on one device may be relied on, other than what follows from the above.
Results may differ from the reference program's by a relative error of at most 0.02.
Values may be sent and summed in bfloat16 or wider, within the bound.
No kernel may reach another device: no remote copies, remote signals or barrier semaphores. Data moves between devices by JAX's collectives and lax.ppermute only.
A program may use at most 64 MiB of HBM per device.

```python
import math
import jax
import jax.numpy as jnp
from jax import lax

CHANNELS = 4096
TAPS = 16
BEAMS = 128
POLS = 2
FIRST = 4
SPECTRA = 4
SECOND = 1024
STATIONS = 512
SAMPLES = 77824
N_GRP = 16
N_CHAN = 32


def set_ends(values, rng, low, largest):
    longest = values.shape.index(max(values.shape))
    spots = []
    for shift in (0, 1):
        where = [jax.random.randint(jax.random.fold_in(rng, axis), (), 0, length) for axis, length in enumerate(values.shape)]
        where[longest] = (where[longest] + shift) % values.shape[longest]
        spots.append(tuple(where))
    return values.at[spots[0]].set(low).at[spots[1]].set(largest)


def shard_levels(own_key, shape, pieces, low, largest):
    def one(dim, shards_of):
        steps = jax.random.uniform(jax.random.fold_in(jax.random.fold_in(own_key, 6), dim), (shards_of,), jnp.float32, low / len(pieces), largest / len(pieces))
        return jnp.repeat(jnp.exp(steps), shape[dim] // shards_of).reshape((-1,) + (1,) * (len(shape) - dim - 1))

    gain = one(*pieces[0])
    for cut in pieces[1:]:
        gain = gain * one(*cut)
    return gain


def gaussian(stream_key, shape, scale, limit, shards=(), held_as=jnp.bfloat16):
    values = scale * jax.random.normal(stream_key, shape, jnp.float32)
    if shards:
        values = values * shard_levels(stream_key, shape, shards, -0.22, 0.18)
    return jnp.clip(values, -limit, limit).astype(held_as)


def setup_inputs(seed: int = 0) -> dict:
    key_of = jax.random.split(jax.random.key(seed), 5)
    voltages = gaussian(key_of[0], (STATIONS, POLS, 2, SAMPLES), 1.0, 6.0, ((0, 512),))
    beam_weights = gaussian(key_of[1], (STATIONS, CHANNELS, 2, BEAMS), STATIONS ** -0.5, 0.25, ((0, 16), (1, 32)))
    owner_table = jax.random.permutation(key_of[2], CHANNELS).astype(jnp.int32)
    live_stations = set_ends((jax.random.randint(key_of[3], (STATIONS,), 0, 8) < 7).astype(jnp.int32), jax.random.fold_in(key_of[3], 1), 0, 1)
    return dict(voltages=voltages, beam_weights=beam_weights, owner_table=owner_table, live_stations=live_stations)


def prototype():
    total = TAPS * CHANNELS
    place = jnp.arange(total, dtype=jnp.int32).astype(jnp.float32)
    window = 0.54 - 0.46 * jnp.cos(2.0 * math.pi * place / total)
    centred = (place - float(total // 2)) / CHANNELS
    return (window * jnp.sinc(centred) / math.sqrt(CHANNELS)).reshape(TAPS, CHANNELS)

def section_table(length, modulus, dtype):
    points = jnp.arange(length, dtype=jnp.int32)
    angle = 2.0 * math.pi * (points[:, None] * points[None, :] % modulus).astype(jnp.float32) / modulus
    cosine = jnp.cos(angle).astype(dtype)
    sine = jnp.sin(angle).astype(dtype)
    return jnp.stack([jnp.stack([cosine, -sine], 1), jnp.stack([sine, cosine], 1)], 0)

def channelize(volts):
    stations = volts.shape[0]
    frames = volts.reshape(stations, POLS, 2, SPECTRA + TAPS - 1, CHANNELS)
    coeffs = prototype()
    summed = jnp.zeros((stations, POLS, 2, SPECTRA, CHANNELS), jnp.float32)
    for tap_index in range(TAPS):
        summed = summed + frames[:, :, :, tap_index:tap_index + SPECTRA, :].astype(jnp.float32) * coeffs[tap_index]
    filtered = lax.optimization_barrier(summed.astype(jnp.bfloat16))
    split = filtered.astype(jnp.float32).reshape(stations, POLS, 2, SPECTRA, FIRST, SECOND)
    first_table = section_table(FIRST, FIRST, jnp.float32)
    folded = jnp.einsum('gprsnm,rnqk->gpqskm', split, first_table, precision=lax.Precision.HIGHEST)
    low = jnp.arange(FIRST, dtype=jnp.int32)
    high = jnp.arange(SECOND, dtype=jnp.int32)
    angle = 2.0 * math.pi * (low[:, None] * high[None, :] % CHANNELS).astype(jnp.float32) / CHANNELS
    cosine = jnp.cos(angle)
    sine = jnp.sin(angle)
    real_in = folded[:, :, 0]
    imag_in = folded[:, :, 1]
    twisted = jnp.stack([real_in * cosine + imag_in * sine, imag_in * cosine - real_in * sine], 2)
    twisted = lax.optimization_barrier(twisted.astype(jnp.bfloat16)).astype(jnp.float32)
    second_table = lax.optimization_barrier(section_table(SECOND, SECOND, jnp.bfloat16)).astype(jnp.float32)
    spectra = jnp.einsum('gprskn,rnqm->gpsqkm', twisted, second_table, precision=lax.Precision.HIGHEST)
    return spectra.reshape(stations, POLS, SPECTRA, 2, CHANNELS).astype(jnp.bfloat16)

def reference(voltages, beam_weights, owner_table, live_stations):
    slot_index = (owner_table % FIRST * SECOND + owner_table // FIRST).astype(jnp.int32)
    group_volts = voltages.reshape(N_GRP, N_CHAN, POLS, 2, SAMPLES)
    group_weights = beam_weights.reshape(N_GRP, N_CHAN, CHANNELS, 2, BEAMS)
    group_live = live_stations.reshape(N_GRP, N_CHAN)

    def one_group(running, inputs):
        volts, weights, alive = inputs
        spectra = channelize(volts)
        spectra = jnp.take(spectra, slot_index, axis=4) * alive.astype(jnp.bfloat16)[:, None, None, None, None]
        values = spectra.astype(jnp.float32)
        factors = weights.astype(jnp.float32)
        real_part = jnp.einsum('tpsc,tcb->bpsc', values[:, :, :, 0], factors[:, :, 0]) - jnp.einsum('tpsc,tcb->bpsc', values[:, :, :, 1], factors[:, :, 1])
        imag_part = jnp.einsum('tpsc,tcb->bpsc', values[:, :, :, 0], factors[:, :, 1]) + jnp.einsum('tpsc,tcb->bpsc', values[:, :, :, 1], factors[:, :, 0])
        partial_value = lax.optimization_barrier(jnp.stack([real_part, imag_part], 1).astype(jnp.bfloat16))
        return (running + partial_value.astype(jnp.float32), None)
    start_value = jnp.zeros((BEAMS, 2, POLS, SPECTRA, CHANNELS), jnp.float32)
    result, unused = lax.scan(one_group, start_value, (group_volts, group_weights, group_live))
    return result
```

```python
import functools

import jax
import jax.numpy as jnp
import numpy as np
from jax import lax
from jax.experimental import pallas as pl
from jax.experimental.pallas import tpu as pltpu
from jax.sharding import PartitionSpec as P

CHANNELS = 4096
TAPS = 16
BEAMS = 128
POLS = 2
SPECTRA = 4
FRAMES = SPECTRA + TAPS - 1
LANES = 128
FIRST = CHANNELS // LANES
ROWS = 2 * FIRST
PARTS = 2 * POLS * SPECTRA
HALF = FIRST // 2
WIDE = 8


def tap_rows():
    total = TAPS * CHANNELS
    place = np.arange(total, dtype=np.float64)
    window = 0.54 - 0.46 * np.cos(2.0 * np.pi * place / total)
    taps = window * np.sinc((place - total // 2) / CHANNELS) / np.sqrt(CHANNELS)
    taps = taps.reshape(TAPS, FIRST, 1, LANES)
    return np.broadcast_to(taps, (TAPS, FIRST, 2, LANES)).reshape(TAPS, ROWS, LANES)


def first_matrix():
    k, q = np.arange(FIRST)[:, None], np.arange(FIRST)[None, :]
    angle = 2.0 * np.pi * (k * q % FIRST) / FIRST
    cosine, sine = np.cos(angle), np.sin(angle)
    real = np.stack([cosine, sine], 2).reshape(FIRST, ROWS)
    imag = np.stack([-sine, cosine], 2).reshape(FIRST, ROWS)
    whole = np.concatenate([real, imag], 0)
    high = whole.astype(jnp.bfloat16)
    low = (whole - high.astype(np.float64)).astype(jnp.bfloat16)
    return np.concatenate([high, low], 1)


def twiddles():
    k, n = np.arange(FIRST)[:, None], np.arange(LANES)[None, :]
    angle = 2.0 * np.pi * (k * n) / CHANNELS
    return np.stack([np.cos(angle), np.sin(angle)], 0).astype(np.float32)


def second_matrix():
    n, m = np.arange(LANES)[:, None], np.arange(LANES)[None, :]
    angle = 2.0 * np.pi * (n * m % LANES) / LANES
    cosine, sine = np.cos(angle), np.sin(angle)
    return np.block([[cosine, -sine], [sine, cosine]]).astype(jnp.bfloat16)


def spread_matrix(stations):
    out = np.zeros((POLS, 2, stations, 2, POLS, stations, WIDE, 2), np.float32)
    for p in range(POLS):
        for st in range(stations):
            out[p, 0, st, 0, p, st, :, 0] = 1.0
            out[p, 1, st, 0, p, st, :, 1] = -1.0
            out[p, 1, st, 1, p, st, :, 0] = 1.0
            out[p, 0, st, 1, p, st, :, 1] = 1.0
    return out.reshape(POLS * 2 * stations, 4 * stations * WIDE * 2).astype(jnp.bfloat16)


def channel_kernel(v_ref, owner_ref, live_ref, taps_ref, first_ref, turn_ref, second_ref, out_ref, folded_ref):
    f32, bf16 = jnp.float32, jnp.bfloat16
    step = 16
    filtered = [[None] * (ROWS // step) for _ in range(POLS * SPECTRA)]
    for p in range(POLS):
        for c in range(ROWS // step):
            sums = [None] * SPECTRA
            for u in range(FRAMES):
                x = v_ref[p, u * ROWS + c * step : u * ROWS + (c + 1) * step, :].astype(f32)
                for s in range(SPECTRA):
                    t = u - s
                    if 0 <= t < TAPS:
                        term = x * taps_ref[t, c * step : (c + 1) * step, :]
                        sums[s] = term if sums[s] is None else sums[s] + term
            for s in range(SPECTRA):
                filtered[p * SPECTRA + s][c] = sums[s].astype(bf16)
    columns = jnp.concatenate([jnp.concatenate(rows, 0) for rows in filtered], 1)
    first = jnp.dot(
        first_ref[...], jnp.concatenate([columns, columns], 0), preferred_element_type=f32
    )
    cosine, sine = turn_ref[0], turn_ref[1]
    count = POLS * SPECTRA
    for i in range(count):
        real = first[:FIRST, i * LANES : (i + 1) * LANES]
        imag = first[FIRST:, i * LANES : (i + 1) * LANES]
        folded_ref[0, pl.ds(i, FIRST, stride=count), :] = real * cosine + imag * sine
        folded_ref[1, pl.ds(i, FIRST, stride=count), :] = imag * cosine - real * sine
    folded = jnp.concatenate([folded_ref[0], folded_ref[1]], 1).astype(bf16)
    spectrum = jnp.dot(folded, second_ref[...], preferred_element_type=f32)
    spectrum = spectrum.astype(bf16).astype(f32) * live_ref[0].astype(f32)
    cut = HALF * count
    table = jnp.concatenate(
        [
            jnp.concatenate([spectrum[:cut, :LANES], spectrum[cut:, :LANES]], 1),
            jnp.concatenate([spectrum[:cut, LANES:], spectrum[cut:, LANES:]], 1),
        ],
        0,
    ).astype(bf16)
    rows = lax.broadcasted_iota(jnp.int32, (2 * LANES, LANES), 0)
    for c in range(out_ref.shape[0] // 2):
        picks = []
        lows = []
        for d in range(2):
            owner = owner_ref[2 * c + d : 2 * c + d + 1, :]
            key = ((owner >> 4) & 1) * LANES + (owner >> 5)
            picks.append(jnp.where(rows == key, 1.0, 0.0).astype(bf16))
            lows.append(jnp.broadcast_to(owner & 15, (count, LANES)))
        found = jnp.dot(table, jnp.concatenate(picks, 1), preferred_element_type=f32)
        for d in range(2):
            parts = []
            for r in range(2):
                block = found[r * cut : (r + 1) * cut, d * LANES : (d + 1) * LANES]
                total = block[:count]
                for h in range(1, HALF):
                    total = jnp.where(lows[d] == h, block[h * count : (h + 1) * count], total)
                parts.append(total)
            out_ref[2 * c + d] = jnp.concatenate(parts, 0).astype(bf16)


def channelize(volts, owner_table, live):
    volts = volts.reshape(POLS, 2, FRAMES * FIRST, LANES)
    volts = jnp.transpose(volts, (0, 2, 1, 3)).reshape(POLS, FRAMES * ROWS, LANES)
    owner = owner_table.reshape(CHANNELS // LANES, LANES)
    vmem = pl.BlockSpec(memory_space=pltpu.VMEM)
    return pl.pallas_call(
        channel_kernel,
        out_shape=jax.ShapeDtypeStruct((CHANNELS // LANES, PARTS, LANES), jnp.bfloat16),
        in_specs=[vmem, vmem, pl.BlockSpec(memory_space=pltpu.SMEM)] + [vmem] * 4,
        out_specs=vmem,
        scratch_shapes=[pltpu.VMEM((2, FIRST * POLS * SPECTRA, LANES), jnp.float32)],
        compiler_params=pltpu.CompilerParams(vmem_limit_bytes=24 * 2**20),
        name="channelize",
    )(
        volts,
        owner,
        live,
        jnp.asarray(tap_rows(), jnp.float32),
        jnp.asarray(first_matrix()),
        jnp.asarray(twiddles()),
        jnp.asarray(second_matrix()),
    )


def beam_kernel(x_ref, w_hbm, spread_ref, out_ref, w_ref, wide_ref, sem):
    f32, bf16 = jnp.float32, jnp.bfloat16
    stations = x_ref.shape[0]
    groups = LANES // WIDE
    copies = []
    for g in range(groups):
        here = pl.ds(g * 2 * WIDE, 2 * WIDE)
        copies.append(pltpu.make_async_copy(w_hbm.at[:, here, :], w_ref.at[g], sem.at[g]))
        copies[-1].start()
    wide_ref[...] = x_ref[...].reshape(stations * PARTS, LANES).astype(f32)
    turned = []
    for s in range(SPECTRA):
        rows = []
        for p in range(POLS):
            for r in range(2):
                start = r * POLS * SPECTRA + p * SPECTRA + s
                rows.append(wide_ref[pl.ds(start, stations, stride=PARTS), :])
        turned.append(jnp.concatenate(rows, 0).T)
    depth = stations * WIDE * 2
    row_slot = lax.broadcasted_iota(jnp.int32, (SPECTRA * WIDE, depth), 0) % WIDE
    column_slot = lax.broadcasted_iota(jnp.int32, (SPECTRA * WIDE, depth), 1) // 2 % WIDE
    meets = row_slot == column_slot
    together = 4
    height = SPECTRA * WIDE
    for batch in range(groups // together):
        small = []
        for g in range(batch * together, (batch + 1) * together):
            for s in range(SPECTRA):
                small.append(turned[s][g * WIDE : (g + 1) * WIDE])
        spread = jnp.dot(
            jnp.concatenate(small, 0).astype(bf16), spread_ref[...], preferred_element_type=f32
        )
        beams = []
        for i in range(together):
            g = batch * together + i
            lhs = jnp.concatenate(
                [
                    jnp.where(
                        meets,
                        spread[i * height : (i + 1) * height, b * depth : (b + 1) * depth],
                        0.0,
                    ).astype(bf16)
                    for b in range(2 * POLS)
                ],
                0,
            )
            copies[g].wait()
            product = jnp.dot(
                lhs, w_ref[g].reshape(depth, BEAMS), preferred_element_type=f32
            )
            beams.append(product.T)
        for pair in range(together // 2):
            where = (batch * together // 2 + pair) * 16
            for b in range(out_ref.shape[0]):
                out_ref[b, where : where + 16, :] = jnp.concatenate(
                    [beams[2 * pair + d][8 * b : 8 * b + 8] for d in range(2)], 0
                ).astype(bf16)


def beamform(spectra, weights):
    stations = weights.shape[0]
    groups = LANES // WIDE
    vmem = pl.BlockSpec(memory_space=pltpu.VMEM)
    weights = weights.reshape(stations, LANES * 2, BEAMS)
    return pl.pallas_call(
        beam_kernel,
        out_shape=jax.ShapeDtypeStruct((BEAMS // 8, 8 * groups, LANES), jnp.bfloat16),
        in_specs=[vmem, pl.BlockSpec(memory_space=pl.ANY), vmem],
        out_specs=vmem,
        scratch_shapes=[
            pltpu.VMEM((groups, stations, 2 * WIDE, BEAMS), jnp.bfloat16),
            pltpu.VMEM((stations * PARTS, LANES), jnp.float32),
            pltpu.SemaphoreType.DMA((groups,)),
        ],
        compiler_params=pltpu.CompilerParams(vmem_limit_bytes=24 * 2**20),
        name="beamform",
    )(spectra, weights, jnp.asarray(spread_matrix(stations)))


def sum_kernel(x_ref, out_ref):
    f32 = jnp.float32
    groups = LANES // WIDE
    held = []
    for g in range(0, groups, 2):
        total = x_ref[0, 8 * g : 8 * g + 16, :].astype(f32)
        for source in range(1, x_ref.shape[0]):
            total = total + x_ref[source, 8 * g : 8 * g + 16, :].astype(f32)
        held += [total[:8], total[8:]]
    block = lax.broadcasted_iota(jnp.int32, (8, LANES), 1) // WIDE
    bit = 1
    while bit < groups:
        upper = (block & bit) != 0
        for i in range(groups):
            if i & bit:
                continue
            low, high = held[i], held[i | bit]
            held[i] = jnp.where(upper, pltpu.roll(high, WIDE * bit, 1), low)
            held[i | bit] = jnp.where(upper, high, pltpu.roll(low, LANES - WIDE * bit, 1))
        bit *= 2
    for i in range(groups):
        r, p, s = i // (POLS * SPECTRA), i // SPECTRA % POLS, i % SPECTRA
        out_ref[:, r, p, s, :] = held[i]


def total(parts):
    vmem = pl.BlockSpec(memory_space=pltpu.VMEM)
    return pl.pallas_call(
        sum_kernel,
        out_shape=jax.ShapeDtypeStruct((8, 2, POLS, SPECTRA, LANES), jnp.float32),
        in_specs=[vmem],
        out_specs=vmem,
        name="sum_groups",
    )(parts)


def shards(voltages, beam_weights, owner_table, live_stations):
    spectra = channelize(voltages, owner_table, live_stations)
    turned = lax.all_to_all(spectra, "chan", split_axis=0, concat_axis=0, tiled=True)
    partial = beamform(turned, beam_weights)
    gathered = lax.all_to_all(partial, "grp", split_axis=0, concat_axis=0, tiled=True)
    return total(gathered)


def solution(mesh):
    in_specs = (
        P(("grp", "chan"), None, None, None),
        P("grp", "chan", None, None),
        P(),
        P(("grp", "chan")),
    )
    out_specs = P("grp", None, None, None, "chan")
    return jax.shard_map(shards, mesh=mesh, in_specs=in_specs, out_specs=out_specs, check_vma=False)
```

```python
import functools

import jax
import jax.numpy as jnp
import numpy as np
from jax import lax
from jax.experimental import pallas as pl
from jax.experimental.pallas import tpu as pltpu
from jax.sharding import PartitionSpec as P

CHANNELS = 4096
TAPS = 16
BEAMS = 128
POLS = 2
SPECTRA = 4
FRAMES = SPECTRA + TAPS - 1
LANES = 128
FIRST = CHANNELS // LANES
ROWS = 2 * FIRST
PARTS = 2 * POLS * SPECTRA
HALF = FIRST // 2
WIDE = 8


def tap_rows():
    total = TAPS * CHANNELS
    place = np.arange(total, dtype=np.float64)
    window = 0.54 - 0.46 * np.cos(2.0 * np.pi * place / total)
    taps = window * np.sinc((place - total // 2) / CHANNELS) / np.sqrt(CHANNELS)
    taps = taps.reshape(TAPS, FIRST, 1, LANES)
    return np.broadcast_to(taps, (TAPS, FIRST, 2, LANES)).reshape(TAPS, ROWS, LANES)


def first_matrix():
    k, q = np.arange(FIRST)[:, None], np.arange(FIRST)[None, :]
    angle = 2.0 * np.pi * (k * q % FIRST) / FIRST
    cosine, sine = np.cos(angle), np.sin(angle)
    real = np.stack([cosine, sine], 2).reshape(FIRST, ROWS)
    imag = np.stack([-sine, cosine], 2).reshape(FIRST, ROWS)
    whole = np.concatenate([real, imag], 0)
    high = whole.astype(jnp.bfloat16)
    low = (whole - high.astype(np.float64)).astype(jnp.bfloat16)
    return np.concatenate([high, low], 1)


def twiddles():
    k, n = np.arange(FIRST)[:, None], np.arange(LANES)[None, :]
    angle = 2.0 * np.pi * (k * n) / CHANNELS
    return np.stack([np.cos(angle), np.sin(angle)], 0).astype(np.float32)


def second_matrix():
    n, m = np.arange(LANES)[:, None], np.arange(LANES)[None, :]
    angle = 2.0 * np.pi * (n * m % LANES) / LANES
    cosine, sine = np.cos(angle), np.sin(angle)
    return np.block([[cosine, -sine], [sine, cosine]]).astype(jnp.bfloat16)


def spread_matrix(stations):
    out = np.zeros((POLS, 2, stations, 2, POLS, stations, WIDE, 2), np.float32)
    for p in range(POLS):
        for st in range(stations):
            out[p, 0, st, 0, p, st, :, 0] = 1.0
            out[p, 1, st, 0, p, st, :, 1] = -1.0
            out[p, 1, st, 1, p, st, :, 0] = 1.0
            out[p, 0, st, 1, p, st, :, 1] = 1.0
    return out.reshape(POLS * 2 * stations, 4 * stations * WIDE * 2).astype(jnp.bfloat16)


def channel_kernel(
    v_hbm,
    owner_hbm,
    live_ref,
    taps_hbm,
    first_hbm,
    turn_hbm,
    second_hbm,
    w_hbm,
    spread_hbm,
    out_ref,
    w_ref,
    spread_ref,
    v_ref,
    owner_ref,
    taps_ref,
    first_ref,
    turn_ref,
    second_ref,
    pick_ref,
    folded_ref,
    sem,
):
    f32, bf16 = jnp.float32, jnp.bfloat16
    pairs = [
        (owner_hbm, owner_ref),
        (taps_hbm, taps_ref),
        (v_hbm.at[0], v_ref.at[0]),
        (v_hbm.at[1], v_ref.at[1]),
        (first_hbm, first_ref),
        (turn_hbm, turn_ref),
        (second_hbm, second_ref),
        (spread_hbm, spread_ref),
        (w_hbm, w_ref),
    ]
    copies = [pltpu.make_async_copy(a, b, sem.at[i]) for i, (a, b) in enumerate(pairs)]
    for copy in copies:
        copy.start()
    blocks = out_ref.shape[0]
    count = POLS * SPECTRA

    copies[0].wait()
    rows = lax.broadcasted_iota(jnp.int32, (2 * LANES, LANES), 0)
    for c in range(blocks):
        owner = owner_ref[c : c + 1, :]
        key = ((owner >> 4) & 1) * LANES + (owner >> 5)
        pick_ref[:, c * LANES : (c + 1) * LANES] = jnp.where(rows == key, 1.0, 0.0).astype(bf16)

    copies[1].wait()
    step = 16
    filtered = [[None] * (ROWS // step) for _ in range(count)]
    for p in range(POLS):
        copies[2 + p].wait()
        for c in range(ROWS // step):
            sums = [None] * SPECTRA
            for u in range(FRAMES):
                x = v_ref[p, u * ROWS + c * step : u * ROWS + (c + 1) * step, :].astype(f32)
                for s in range(SPECTRA):
                    t = u - s
                    if 0 <= t < TAPS:
                        term = x * taps_ref[t, c * step : (c + 1) * step, :]
                        sums[s] = term if sums[s] is None else sums[s] + term
            for s in range(SPECTRA):
                filtered[p * SPECTRA + s][c] = sums[s].astype(bf16)
    columns = jnp.concatenate([jnp.concatenate(rows, 0) for rows in filtered], 1)
    copies[4].wait()
    first = jnp.dot(
        first_ref[...], jnp.concatenate([columns, columns], 0), preferred_element_type=f32
    )
    copies[5].wait()
    cosine, sine = turn_ref[0], turn_ref[1]
    for i in range(count):
        real = first[:FIRST, i * LANES : (i + 1) * LANES]
        imag = first[FIRST:, i * LANES : (i + 1) * LANES]
        folded_ref[0, pl.ds(i, FIRST, stride=count), :] = real * cosine + imag * sine
        folded_ref[1, pl.ds(i, FIRST, stride=count), :] = imag * cosine - real * sine
    folded = jnp.concatenate([folded_ref[0], folded_ref[1]], 1).astype(bf16)
    copies[6].wait()
    spectrum = jnp.dot(folded, second_ref[...], preferred_element_type=f32)
    spectrum = spectrum.astype(bf16).astype(f32) * live_ref[0].astype(f32)
    cut = HALF * count
    table = jnp.concatenate(
        [
            jnp.concatenate([spectrum[:cut, :LANES], spectrum[cut:, :LANES]], 1),
            jnp.concatenate([spectrum[:cut, LANES:], spectrum[cut:, LANES:]], 1),
        ],
        0,
    ).astype(bf16)
    for c in range(0, blocks, 2):
        found = jnp.dot(
            table, pick_ref[:, c * LANES : (c + 2) * LANES], preferred_element_type=f32
        )
        for d in range(2):
            low = jnp.broadcast_to(owner_ref[c + d : c + d + 1, :] & 15, (count, LANES))
            parts = []
            for r in range(2):
                block = found[r * cut : (r + 1) * cut, d * LANES : (d + 1) * LANES]
                total = block[:count]
                for h in range(1, HALF):
                    total = jnp.where(low == h, block[h * count : (h + 1) * count], total)
                parts.append(total)
            out_ref[c + d] = jnp.concatenate(parts, 0).astype(bf16)
    copies[7].wait()
    copies[8].wait()


def place(array):
    return pltpu.with_memory_space_constraint(array, pltpu.HBM)


def channelize(volts, owner_table, live, weights):
    volts = volts.reshape(POLS, 2, FRAMES * FIRST, LANES)
    volts = jnp.transpose(volts, (0, 2, 1, 3)).reshape(POLS, FRAMES * ROWS, LANES)
    owner = owner_table.reshape(CHANNELS // LANES, LANES)
    stations = weights.shape[0]
    weights = weights.reshape(stations, LANES * 2, BEAMS)
    constants = [
        jnp.asarray(tap_rows(), jnp.float32),
        jnp.asarray(first_matrix()),
        jnp.asarray(twiddles()),
        jnp.asarray(second_matrix()),
    ]
    spread = jnp.asarray(spread_matrix(stations))
    vmem = pl.BlockSpec(memory_space=pltpu.VMEM)
    hbm = pl.BlockSpec(memory_space=pltpu.HBM)
    held = [pltpu.VMEM(a.shape, a.dtype) for a in [volts, owner] + constants]
    return pl.pallas_call(
        channel_kernel,
        out_shape=[
            jax.ShapeDtypeStruct((CHANNELS // LANES, PARTS, LANES), jnp.bfloat16),
            jax.ShapeDtypeStruct(weights.shape, jnp.bfloat16),
            jax.ShapeDtypeStruct(spread.shape, jnp.bfloat16),
        ],
        in_specs=[hbm, hbm, pl.BlockSpec(memory_space=pltpu.SMEM)] + [hbm] * 6,
        out_specs=[vmem] * 3,
        scratch_shapes=held
        + [
            pltpu.VMEM((2 * LANES, CHANNELS), jnp.bfloat16),
            pltpu.VMEM((2, FIRST * POLS * SPECTRA, LANES), jnp.float32),
            pltpu.SemaphoreType.DMA((9,)),
        ],
        compiler_params=pltpu.CompilerParams(vmem_limit_bytes=20 * 2**20),
        name="channelize",
    )(*[place(a) for a in (volts, owner)], live, *[place(a) for a in constants + [weights, spread]])


def beam_kernel(x_ref, w_ref, spread_ref, out_ref, wide_ref):
    f32, bf16 = jnp.float32, jnp.bfloat16
    stations = x_ref.shape[0]
    groups = LANES // WIDE
    wide_ref[...] = x_ref[...].reshape(stations * PARTS, LANES).astype(f32)
    turned = []
    for s in range(SPECTRA):
        rows = []
        for p in range(POLS):
            for r in range(2):
                start = r * POLS * SPECTRA + p * SPECTRA + s
                rows.append(wide_ref[pl.ds(start, stations, stride=PARTS), :])
        turned.append(jnp.concatenate(rows, 0).T)
    depth = stations * WIDE * 2
    row_slot = lax.broadcasted_iota(jnp.int32, (SPECTRA * WIDE, depth), 0) % WIDE
    column_slot = lax.broadcasted_iota(jnp.int32, (SPECTRA * WIDE, depth), 1) // 2 % WIDE
    meets = row_slot == column_slot
    together = 4
    height = SPECTRA * WIDE
    for batch in range(groups // together):
        small = []
        for g in range(batch * together, (batch + 1) * together):
            for s in range(SPECTRA):
                small.append(turned[s][g * WIDE : (g + 1) * WIDE])
        spread = jnp.dot(
            jnp.concatenate(small, 0).astype(bf16), spread_ref[...], preferred_element_type=f32
        )
        beams = []
        for i in range(together):
            g = batch * together + i
            lhs = jnp.concatenate(
                [
                    jnp.where(
                        meets,
                        spread[i * height : (i + 1) * height, b * depth : (b + 1) * depth],
                        0.0,
                    ).astype(bf16)
                    for b in range(2 * POLS)
                ],
                0,
            )
            weights = w_ref[:, g * 2 * WIDE : (g + 1) * 2 * WIDE, :].reshape(depth, BEAMS)
            product = jnp.dot(lhs, weights, preferred_element_type=f32)
            beams.append(product.T)
        for pair in range(together // 2):
            where = (batch * together // 2 + pair) * 16
            for b in range(out_ref.shape[0]):
                out_ref[b, where : where + 16, :] = jnp.concatenate(
                    [beams[2 * pair + d][8 * b : 8 * b + 8] for d in range(2)], 0
                ).astype(bf16)


def beamform(spectra, weights, spread):
    stations = weights.shape[0]
    groups = LANES // WIDE
    vmem = pl.BlockSpec(memory_space=pltpu.VMEM)
    return pl.pallas_call(
        beam_kernel,
        out_shape=jax.ShapeDtypeStruct((BEAMS // 8, 8 * groups, LANES), jnp.bfloat16),
        in_specs=[vmem] * 3,
        out_specs=vmem,
        scratch_shapes=[pltpu.VMEM((stations * PARTS, LANES), jnp.float32)],
        compiler_params=pltpu.CompilerParams(vmem_limit_bytes=20 * 2**20),
        name="beamform",
    )(spectra, weights, spread)


def sum_kernel(x_ref, out_ref):
    f32 = jnp.float32
    groups = LANES // WIDE
    held = []
    for g in range(0, groups, 2):
        total = x_ref[0, 8 * g : 8 * g + 16, :].astype(f32)
        for source in range(1, x_ref.shape[0]):
            total = total + x_ref[source, 8 * g : 8 * g + 16, :].astype(f32)
        held += [total[:8], total[8:]]
    block = lax.broadcasted_iota(jnp.int32, (8, LANES), 1) // WIDE
    bit = 1
    while bit < groups:
        upper = (block & bit) != 0
        for i in range(groups):
            if i & bit:
                continue
            low, high = held[i], held[i | bit]
            held[i] = jnp.where(upper, pltpu.roll(high, WIDE * bit, 1), low)
            held[i | bit] = jnp.where(upper, high, pltpu.roll(low, LANES - WIDE * bit, 1))
        bit *= 2
    for i in range(groups):
        r, p, s = i // (POLS * SPECTRA), i // SPECTRA % POLS, i % SPECTRA
        out_ref[:, r, p, s, :] = held[i]


def total(parts):
    vmem = pl.BlockSpec(memory_space=pltpu.VMEM)
    return pl.pallas_call(
        sum_kernel,
        out_shape=jax.ShapeDtypeStruct((8, 2, POLS, SPECTRA, LANES), jnp.float32),
        in_specs=[vmem],
        out_specs=vmem,
        compiler_params=pltpu.CompilerParams(vmem_limit_bytes=20 * 2**20),
        name="sum_groups",
    )(parts)


def shards(voltages, beam_weights, owner_table, live_stations):
    spectra, weights, spread = channelize(voltages, owner_table, live_stations, beam_weights)
    turned = lax.all_to_all(spectra, "chan", split_axis=0, concat_axis=0, tiled=True)
    partial = beamform(turned, weights, spread)
    gathered = lax.all_to_all(partial, "grp", split_axis=0, concat_axis=0, tiled=True)
    return total(gathered)


def solution(mesh):
    in_specs = (
        P(("grp", "chan"), None, None, None),
        P("grp", "chan", None, None),
        P(),
        P(("grp", "chan")),
    )
    out_specs = P("grp", None, None, None, "chan")
    return jax.shard_map(shards, mesh=mesh, in_specs=in_specs, out_specs=out_specs, check_vma=False)
```

```python
import functools

import jax
import jax.numpy as jnp
import numpy as np
from jax import lax
from jax.experimental import pallas as pl
from jax.experimental.pallas import tpu as pltpu
from jax.sharding import PartitionSpec as P

CHANNELS = 4096
TAPS = 16
BEAMS = 128
POLS = 2
SPECTRA = 4
FRAMES = SPECTRA + TAPS - 1
LANES = 128
FIRST = CHANNELS // LANES
ROWS = 2 * FIRST
PARTS = 2 * POLS * SPECTRA
HALF = FIRST // 2
WIDE = 8
CHAN_LEAD = 30
GRP_LEAD = 10


def leading(first, count):
    return [first] + [i for i in range(count) if i != first]


def tap_rows():
    total = TAPS * CHANNELS
    place = np.arange(total, dtype=np.float64)
    window = 0.54 - 0.46 * np.cos(2.0 * np.pi * place / total)
    taps = window * np.sinc((place - total // 2) / CHANNELS) / np.sqrt(CHANNELS)
    taps = taps.reshape(TAPS, FIRST, 1, LANES)
    return np.broadcast_to(taps, (TAPS, FIRST, 2, LANES)).reshape(TAPS, ROWS, LANES)


def first_matrix():
    k, q = np.arange(FIRST)[:, None], np.arange(FIRST)[None, :]
    angle = 2.0 * np.pi * (k * q % FIRST) / FIRST
    cosine, sine = np.cos(angle), np.sin(angle)
    real = np.stack([cosine, sine], 2).reshape(FIRST, ROWS)
    imag = np.stack([-sine, cosine], 2).reshape(FIRST, ROWS)
    whole = np.concatenate([real, imag], 0)
    high = whole.astype(jnp.bfloat16)
    low = (whole - high.astype(np.float64)).astype(jnp.bfloat16)
    return np.concatenate([high, low], 1)


def twiddles():
    k, n = np.arange(FIRST)[:, None], np.arange(LANES)[None, :]
    angle = 2.0 * np.pi * (k * n) / CHANNELS
    return np.stack([np.cos(angle), np.sin(angle)], 0).astype(np.float32)


def second_matrix():
    n, m = np.arange(LANES)[:, None], np.arange(LANES)[None, :]
    angle = 2.0 * np.pi * (n * m % LANES) / LANES
    cosine, sine = np.cos(angle), np.sin(angle)
    return np.block([[cosine, -sine], [sine, cosine]]).astype(jnp.bfloat16)


def spread_matrix(stations):
    out = np.zeros((POLS, 2, stations, 2, POLS, stations, WIDE, 2), np.float32)
    for p in range(POLS):
        for i, st in enumerate(leading(CHAN_LEAD, stations)):
            out[p, 0, i, 0, p, st, :, 0] = 1.0
            out[p, 1, i, 0, p, st, :, 1] = -1.0
            out[p, 1, i, 1, p, st, :, 0] = 1.0
            out[p, 0, i, 1, p, st, :, 1] = 1.0
    return out.reshape(POLS * 2 * stations, 4 * stations * WIDE * 2).astype(jnp.bfloat16)


def channel_kernel(
    v_hbm,
    owner_hbm,
    live_ref,
    taps_hbm,
    first_hbm,
    turn_hbm,
    second_hbm,
    w_hbm,
    spread_hbm,
    out_ref,
    w_ref,
    spread_ref,
    v_ref,
    owner_ref,
    taps_ref,
    first_ref,
    turn_ref,
    second_ref,
    pick_ref,
    folded_ref,
    sem,
):
    f32, bf16 = jnp.float32, jnp.bfloat16
    pairs = [
        (owner_hbm, owner_ref),
        (taps_hbm, taps_ref),
        (v_hbm.at[0], v_ref.at[0]),
        (v_hbm.at[1], v_ref.at[1]),
        (first_hbm, first_ref),
        (turn_hbm, turn_ref),
        (second_hbm, second_ref),
        (spread_hbm, spread_ref),
        (w_hbm, w_ref),
    ]
    copies = [pltpu.make_async_copy(a, b, sem.at[i]) for i, (a, b) in enumerate(pairs)]
    for copy in copies:
        copy.start()
    blocks = out_ref.shape[0]
    count = POLS * SPECTRA

    copies[0].wait()
    rows = lax.broadcasted_iota(jnp.int32, (2 * LANES, LANES), 0)
    for c in range(blocks):
        owner = owner_ref[c : c + 1, :]
        key = ((owner >> 4) & 1) * LANES + (owner >> 5)
        pick_ref[:, c * LANES : (c + 1) * LANES] = jnp.where(rows == key, 1.0, 0.0).astype(bf16)

    copies[1].wait()
    step = 16
    filtered = [[None] * (ROWS // step) for _ in range(count)]
    for p in range(POLS):
        copies[2 + p].wait()
        for c in range(ROWS // step):
            sums = [None] * SPECTRA
            for u in range(FRAMES):
                x = v_ref[p, u * ROWS + c * step : u * ROWS + (c + 1) * step, :].astype(f32)
                for s in range(SPECTRA):
                    t = u - s
                    if 0 <= t < TAPS:
                        term = x * taps_ref[t, c * step : (c + 1) * step, :]
                        sums[s] = term if sums[s] is None else sums[s] + term
            for s in range(SPECTRA):
                filtered[p * SPECTRA + s][c] = sums[s].astype(bf16)
    columns = jnp.concatenate([jnp.concatenate(rows, 0) for rows in filtered], 1)
    copies[4].wait()
    first = jnp.dot(
        first_ref[...], jnp.concatenate([columns, columns], 0), preferred_element_type=f32
    )
    copies[5].wait()
    cosine, sine = turn_ref[0], turn_ref[1]
    for i in range(count):
        real = first[:FIRST, i * LANES : (i + 1) * LANES]
        imag = first[FIRST:, i * LANES : (i + 1) * LANES]
        folded_ref[0, pl.ds(i, FIRST, stride=count), :] = real * cosine + imag * sine
        folded_ref[1, pl.ds(i, FIRST, stride=count), :] = imag * cosine - real * sine
    folded = jnp.concatenate([folded_ref[0], folded_ref[1]], 1).astype(bf16)
    copies[6].wait()
    spectrum = jnp.dot(folded, second_ref[...], preferred_element_type=f32)
    spectrum = spectrum.astype(bf16).astype(f32) * live_ref[0].astype(f32)
    cut = HALF * count
    table = jnp.concatenate(
        [
            jnp.concatenate([spectrum[:cut, :LANES], spectrum[cut:, :LANES]], 1),
            jnp.concatenate([spectrum[:cut, LANES:], spectrum[cut:, LANES:]], 1),
        ],
        0,
    ).astype(bf16)
    place_of = {c: i for i, c in enumerate(leading(CHAN_LEAD, blocks))}
    for c in range(0, blocks, 2):
        found = jnp.dot(
            table, pick_ref[:, c * LANES : (c + 2) * LANES], preferred_element_type=f32
        )
        for d in range(2):
            low = jnp.broadcast_to(owner_ref[c + d : c + d + 1, :] & 15, (count, LANES))
            parts = []
            for r in range(2):
                block = found[r * cut : (r + 1) * cut, d * LANES : (d + 1) * LANES]
                total = block[:count]
                for h in range(1, HALF):
                    total = jnp.where(low == h, block[h * count : (h + 1) * count], total)
                parts.append(total)
            out_ref[place_of[c + d]] = jnp.concatenate(parts, 0).astype(bf16)
    copies[7].wait()
    copies[8].wait()


def place(array):
    return pltpu.with_memory_space_constraint(array, pltpu.HBM)


def channelize(volts, owner_table, live, weights):
    volts = volts.reshape(POLS, 2, FRAMES * FIRST, LANES)
    volts = jnp.transpose(volts, (0, 2, 1, 3)).reshape(POLS, FRAMES * ROWS, LANES)
    owner = owner_table.reshape(CHANNELS // LANES, LANES)
    stations = weights.shape[0]
    weights = weights.reshape(stations, LANES * 2, BEAMS)
    constants = [
        jnp.asarray(tap_rows(), jnp.float32),
        jnp.asarray(first_matrix()),
        jnp.asarray(twiddles()),
        jnp.asarray(second_matrix()),
    ]
    spread = jnp.asarray(spread_matrix(stations))
    vmem = pl.BlockSpec(memory_space=pltpu.VMEM)
    hbm = pl.BlockSpec(memory_space=pltpu.HBM)
    held = [pltpu.VMEM(a.shape, a.dtype) for a in [volts, owner] + constants]
    return pl.pallas_call(
        channel_kernel,
        out_shape=[
            jax.ShapeDtypeStruct((CHANNELS // LANES, PARTS, LANES), jnp.bfloat16),
            jax.ShapeDtypeStruct(weights.shape, jnp.bfloat16),
            jax.ShapeDtypeStruct(spread.shape, jnp.bfloat16),
        ],
        in_specs=[hbm, hbm, pl.BlockSpec(memory_space=pltpu.SMEM)] + [hbm] * 6,
        out_specs=[vmem] * 3,
        scratch_shapes=held
        + [
            pltpu.VMEM((2 * LANES, CHANNELS), jnp.bfloat16),
            pltpu.VMEM((2, FIRST * POLS * SPECTRA, LANES), jnp.float32),
            pltpu.SemaphoreType.DMA((9,)),
        ],
        compiler_params=pltpu.CompilerParams(vmem_limit_bytes=20 * 2**20),
        name="channelize",
    )(*[place(a) for a in (volts, owner)], live, *[place(a) for a in constants + [weights, spread]])


def beam_kernel(x_ref, w_ref, spread_ref, out_ref, wide_ref):
    f32, bf16 = jnp.float32, jnp.bfloat16
    stations = x_ref.shape[0]
    groups = LANES // WIDE
    wide_ref[...] = x_ref[...].reshape(stations * PARTS, LANES).astype(f32)
    turned = []
    for s in range(SPECTRA):
        rows = []
        for p in range(POLS):
            for r in range(2):
                start = r * POLS * SPECTRA + p * SPECTRA + s
                rows.append(wide_ref[pl.ds(start, stations, stride=PARTS), :])
        turned.append(jnp.concatenate(rows, 0).T)
    depth = stations * WIDE * 2
    row_slot = lax.broadcasted_iota(jnp.int32, (SPECTRA * WIDE, depth), 0) % WIDE
    column_slot = lax.broadcasted_iota(jnp.int32, (SPECTRA * WIDE, depth), 1) // 2 % WIDE
    meets = row_slot == column_slot
    together = 4
    height = SPECTRA * WIDE
    for batch in range(groups // together):
        small = []
        for g in range(batch * together, (batch + 1) * together):
            for s in range(SPECTRA):
                small.append(turned[s][g * WIDE : (g + 1) * WIDE])
        spread = jnp.dot(
            jnp.concatenate(small, 0).astype(bf16), spread_ref[...], preferred_element_type=f32
        )
        beams = []
        for i in range(together):
            g = batch * together + i
            lhs = jnp.concatenate(
                [
                    jnp.where(
                        meets,
                        spread[i * height : (i + 1) * height, b * depth : (b + 1) * depth],
                        0.0,
                    ).astype(bf16)
                    for b in range(2 * POLS)
                ],
                0,
            )
            weights = w_ref[:, g * 2 * WIDE : (g + 1) * 2 * WIDE, :].reshape(depth, BEAMS)
            product = jnp.dot(lhs, weights, preferred_element_type=f32)
            beams.append(product.T)
        for pair in range(together // 2):
            where = (batch * together // 2 + pair) * 16
            for i, b in enumerate(leading(GRP_LEAD, out_ref.shape[0])):
                out_ref[i, where : where + 16, :] = jnp.concatenate(
                    [beams[2 * pair + d][8 * b : 8 * b + 8] for d in range(2)], 0
                ).astype(bf16)


def beamform(spectra, weights, spread):
    stations = weights.shape[0]
    groups = LANES // WIDE
    vmem = pl.BlockSpec(memory_space=pltpu.VMEM)
    return pl.pallas_call(
        beam_kernel,
        out_shape=jax.ShapeDtypeStruct((BEAMS // 8, 8 * groups, LANES), jnp.bfloat16),
        in_specs=[vmem] * 3,
        out_specs=vmem,
        scratch_shapes=[pltpu.VMEM((stations * PARTS, LANES), jnp.float32)],
        compiler_params=pltpu.CompilerParams(vmem_limit_bytes=20 * 2**20),
        name="beamform",
    )(spectra, weights, spread)


def sum_kernel(x_ref, out_ref):
    f32 = jnp.float32
    groups = LANES // WIDE
    held = []
    for g in range(0, groups, 2):
        total = x_ref[0, 8 * g : 8 * g + 16, :].astype(f32)
        for source in range(1, x_ref.shape[0]):
            total = total + x_ref[source, 8 * g : 8 * g + 16, :].astype(f32)
        held += [total[:8], total[8:]]
    block = lax.broadcasted_iota(jnp.int32, (8, LANES), 1) // WIDE
    bit = 1
    while bit < groups:
        upper = (block & bit) != 0
        for i in range(groups):
            if i & bit:
                continue
            low, high = held[i], held[i | bit]
            held[i] = jnp.where(upper, pltpu.roll(high, WIDE * bit, 1), low)
            held[i | bit] = jnp.where(upper, high, pltpu.roll(low, LANES - WIDE * bit, 1))
        bit *= 2
    for i in range(groups):
        r, p, s = i // (POLS * SPECTRA), i // SPECTRA % POLS, i % SPECTRA
        out_ref[:, r, p, s, :] = held[i]


def total(parts):
    vmem = pl.BlockSpec(memory_space=pltpu.VMEM)
    return pl.pallas_call(
        sum_kernel,
        out_shape=jax.ShapeDtypeStruct((8, 2, POLS, SPECTRA, LANES), jnp.float32),
        in_specs=[vmem],
        out_specs=vmem,
        compiler_params=pltpu.CompilerParams(vmem_limit_bytes=20 * 2**20),
        name="sum_groups",
    )(parts)


def exchange(blocks, axis, first):
    order = leading(first, blocks.shape[0])
    return lax.all_to_all(
        blocks, axis, split_axis=0, concat_axis=0, axis_index_groups=[order], tiled=True
    )


def shards(voltages, beam_weights, owner_table, live_stations):
    spectra, weights, spread = channelize(voltages, owner_table, live_stations, beam_weights)
    turned = exchange(spectra, "chan", CHAN_LEAD)
    partial = beamform(turned, weights, spread)
    gathered = exchange(partial, "grp", GRP_LEAD)
    return total(gathered)


def solution(mesh):
    in_specs = (
        P(("grp", "chan"), None, None, None),
        P("grp", "chan", None, None),
        P(),
        P(("grp", "chan")),
    )
    out_specs = P("grp", None, None, None, "chan")
    return jax.shard_map(shards, mesh=mesh, in_specs=in_specs, out_specs=out_specs, check_vma=False)
```

```python
import functools

import jax
import jax.numpy as jnp
import numpy as np
from jax import lax
from jax.experimental import pallas as pl
from jax.experimental.pallas import tpu as pltpu
from jax.sharding import PartitionSpec as P

CHANNELS = 4096
TAPS = 16
BEAMS = 128
POLS = 2
SPECTRA = 4
FRAMES = SPECTRA + TAPS - 1
LANES = 128
FIRST = CHANNELS // LANES
ROWS = 2 * FIRST
PARTS = 2 * POLS * SPECTRA
HALF = FIRST // 2
WIDE = 8
CHAN_LEAD = 30
GRP_LEAD = 10


def leading(first, count):
    return [first] + [i for i in range(count) if i != first]


def tap_rows():
    total = TAPS * CHANNELS
    place = np.arange(total, dtype=np.float64)
    window = 0.54 - 0.46 * np.cos(2.0 * np.pi * place / total)
    taps = window * np.sinc((place - total // 2) / CHANNELS) / np.sqrt(CHANNELS)
    taps = taps.reshape(TAPS, FIRST, 1, LANES)
    return np.broadcast_to(taps, (TAPS, FIRST, 2, LANES)).reshape(TAPS, ROWS, LANES)


def first_matrix():
    k, q = np.arange(FIRST)[:, None], np.arange(FIRST)[None, :]
    angle = 2.0 * np.pi * (k * q % FIRST) / FIRST
    cosine, sine = np.cos(angle), np.sin(angle)
    real = np.stack([cosine, sine], 2).reshape(FIRST, ROWS)
    imag = np.stack([-sine, cosine], 2).reshape(FIRST, ROWS)
    whole = np.concatenate([real, imag], 0)
    high = whole.astype(jnp.bfloat16)
    low = (whole - high.astype(np.float64)).astype(jnp.bfloat16)
    return np.concatenate([high, low], 1)


def twiddles():
    k, n = np.arange(FIRST)[:, None], np.arange(LANES)[None, :]
    angle = 2.0 * np.pi * (k * n) / CHANNELS
    return np.stack([np.cos(angle), np.sin(angle)], 0).astype(np.float32)


def second_matrix():
    n, m = np.arange(LANES)[:, None], np.arange(LANES)[None, :]
    angle = 2.0 * np.pi * (n * m % LANES) / LANES
    cosine, sine = np.cos(angle), np.sin(angle)
    return np.block([[cosine, -sine], [sine, cosine]]).astype(jnp.bfloat16)


def spread_matrix(stations):
    out = np.zeros((POLS, 2, stations, 2, POLS, stations, WIDE, 2), np.float32)
    for p in range(POLS):
        for i, st in enumerate(leading(CHAN_LEAD, stations)):
            out[p, 0, i, 0, p, st, :, 0] = 1.0
            out[p, 1, i, 0, p, st, :, 1] = -1.0
            out[p, 1, i, 1, p, st, :, 0] = 1.0
            out[p, 0, i, 1, p, st, :, 1] = 1.0
    return out.reshape(POLS * 2 * stations, 4 * stations * WIDE * 2).astype(jnp.bfloat16)


def channel_kernel(
    v_hbm,
    owner_hbm,
    live_ref,
    taps_hbm,
    first_hbm,
    turn_hbm,
    second_hbm,
    w_hbm,
    spread_hbm,
    out_ref,
    w_ref,
    spread_ref,
    v_ref,
    owner_ref,
    taps_ref,
    first_ref,
    turn_ref,
    second_ref,
    pick_ref,
    folded_ref,
    sem,
):
    f32, bf16 = jnp.float32, jnp.bfloat16
    pairs = [
        (owner_hbm, owner_ref),
        (taps_hbm, taps_ref),
        (v_hbm.at[0], v_ref.at[0]),
        (v_hbm.at[1], v_ref.at[1]),
        (first_hbm, first_ref),
        (turn_hbm, turn_ref),
        (second_hbm, second_ref),
        (spread_hbm, spread_ref),
        (w_hbm, w_ref),
    ]
    copies = [pltpu.make_async_copy(a, b, sem.at[i]) for i, (a, b) in enumerate(pairs)]
    for copy in copies:
        copy.start()
    blocks = out_ref.shape[0]
    count = POLS * SPECTRA

    copies[0].wait()
    rows = lax.broadcasted_iota(jnp.int32, (2 * LANES, LANES), 0).astype(f32).astype(bf16)
    one, zero = jnp.ones((), bf16), jnp.zeros((), bf16)
    for c in range(blocks):
        owner = owner_ref[c : c + 1, :]
        key = (((owner >> 4) & 1) * LANES + (owner >> 5)).astype(f32).astype(bf16)
        pick_ref[:, c * LANES : (c + 1) * LANES] = jnp.where(rows == key, one, zero)

    copies[1].wait()
    step = 16
    filtered = [[None] * (ROWS // step) for _ in range(count)]
    for p in range(POLS):
        copies[2 + p].wait()
        for c in range(ROWS // step):
            sums = [None] * SPECTRA
            for u in range(FRAMES):
                x = v_ref[p, u * ROWS + c * step : u * ROWS + (c + 1) * step, :].astype(f32)
                for s in range(SPECTRA):
                    t = u - s
                    if 0 <= t < TAPS:
                        term = x * taps_ref[t, c * step : (c + 1) * step, :]
                        sums[s] = term if sums[s] is None else sums[s] + term
            for s in range(SPECTRA):
                filtered[p * SPECTRA + s][c] = sums[s].astype(bf16)
    columns = jnp.concatenate([jnp.concatenate(rows, 0) for rows in filtered], 1)
    copies[4].wait()
    first = jnp.dot(
        first_ref[...], jnp.concatenate([columns, columns], 0), preferred_element_type=f32
    )
    copies[5].wait()
    cosine, sine = turn_ref[0], turn_ref[1]
    for i in range(count):
        real = first[:FIRST, i * LANES : (i + 1) * LANES]
        imag = first[FIRST:, i * LANES : (i + 1) * LANES]
        folded_ref[0, pl.ds(i, FIRST, stride=count), :] = real * cosine + imag * sine
        folded_ref[1, pl.ds(i, FIRST, stride=count), :] = imag * cosine - real * sine
    folded = jnp.concatenate([folded_ref[0], folded_ref[1]], 1).astype(bf16)
    copies[6].wait()
    spectrum = jnp.dot(folded, second_ref[...], preferred_element_type=f32)
    spectrum = spectrum.astype(bf16).astype(f32) * live_ref[0].astype(f32)
    cut = HALF * count
    table = jnp.concatenate(
        [
            jnp.concatenate([spectrum[:cut, :LANES], spectrum[cut:, :LANES]], 1),
            jnp.concatenate([spectrum[:cut, LANES:], spectrum[cut:, LANES:]], 1),
        ],
        0,
    ).astype(bf16)
    place_of = {c: i for i, c in enumerate(leading(CHAN_LEAD, blocks))}
    for c in range(0, blocks, 2):
        found = jnp.dot(
            table, pick_ref[:, c * LANES : (c + 2) * LANES], preferred_element_type=f32
        )
        for d in range(2):
            low = jnp.broadcast_to(owner_ref[c + d : c + d + 1, :] & 15, (count, LANES))
            parts = []
            for r in range(2):
                block = found[r * cut : (r + 1) * cut, d * LANES : (d + 1) * LANES]
                total = block[:count]
                for h in range(1, HALF):
                    total = jnp.where(low == h, block[h * count : (h + 1) * count], total)
                parts.append(total)
            out_ref[place_of[c + d]] = jnp.concatenate(parts, 0).astype(bf16)
    copies[7].wait()
    copies[8].wait()


def place(array):
    return pltpu.with_memory_space_constraint(array, pltpu.HBM)


def channelize(volts, owner_table, live, weights):
    volts = volts.reshape(POLS, 2, FRAMES * FIRST, LANES)
    volts = jnp.transpose(volts, (0, 2, 1, 3)).reshape(POLS, FRAMES * ROWS, LANES)
    owner = owner_table.reshape(CHANNELS // LANES, LANES)
    stations = weights.shape[0]
    weights = weights.reshape(stations, LANES * 2, BEAMS)
    constants = [
        jnp.asarray(tap_rows(), jnp.float32),
        jnp.asarray(first_matrix()),
        jnp.asarray(twiddles()),
        jnp.asarray(second_matrix()),
    ]
    spread = jnp.asarray(spread_matrix(stations))
    vmem = pl.BlockSpec(memory_space=pltpu.VMEM)
    hbm = pl.BlockSpec(memory_space=pltpu.HBM)
    held = [pltpu.VMEM(a.shape, a.dtype) for a in [volts, owner] + constants]
    return pl.pallas_call(
        channel_kernel,
        out_shape=[
            jax.ShapeDtypeStruct((CHANNELS // LANES, PARTS, LANES), jnp.bfloat16),
            jax.ShapeDtypeStruct(weights.shape, jnp.bfloat16),
            jax.ShapeDtypeStruct(spread.shape, jnp.bfloat16),
        ],
        in_specs=[hbm, hbm, pl.BlockSpec(memory_space=pltpu.SMEM)] + [hbm] * 6,
        out_specs=[vmem] * 3,
        scratch_shapes=held
        + [
            pltpu.VMEM((2 * LANES, CHANNELS), jnp.bfloat16),
            pltpu.VMEM((2, FIRST * POLS * SPECTRA, LANES), jnp.float32),
            pltpu.SemaphoreType.DMA((9,)),
        ],
        compiler_params=pltpu.CompilerParams(vmem_limit_bytes=20 * 2**20),
        name="channelize",
    )(*[place(a) for a in (volts, owner)], live, *[place(a) for a in constants + [weights, spread]])


def beam_kernel(x_ref, w_ref, spread_ref, out_ref, wide_ref):
    f32, bf16 = jnp.float32, jnp.bfloat16
    stations = x_ref.shape[0]
    groups = LANES // WIDE
    wide_ref[...] = x_ref[...].reshape(stations * PARTS, LANES).astype(f32)
    turned = []
    for s in range(SPECTRA):
        rows = []
        for p in range(POLS):
            for r in range(2):
                start = r * POLS * SPECTRA + p * SPECTRA + s
                rows.append(wide_ref[pl.ds(start, stations, stride=PARTS), :])
        turned.append(jnp.concatenate(rows, 0).T)
    depth = stations * WIDE * 2
    row_slot = lax.broadcasted_iota(jnp.int32, (SPECTRA * WIDE, depth), 0) % WIDE
    column_slot = lax.broadcasted_iota(jnp.int32, (SPECTRA * WIDE, depth), 1) // 2 % WIDE
    meets = row_slot == column_slot
    together = 16
    height = SPECTRA * WIDE
    for batch in range(groups // together):
        small = []
        for g in range(batch * together, (batch + 1) * together):
            for s in range(SPECTRA):
                small.append(turned[s][g * WIDE : (g + 1) * WIDE])
        spread = jnp.dot(
            jnp.concatenate(small, 0).astype(bf16), spread_ref[...], preferred_element_type=f32
        )
        beams = []
        for i in range(together):
            g = batch * together + i
            lhs = jnp.concatenate(
                [
                    jnp.where(
                        meets,
                        spread[i * height : (i + 1) * height, b * depth : (b + 1) * depth],
                        0.0,
                    ).astype(bf16)
                    for b in range(2 * POLS)
                ],
                0,
            )
            weights = w_ref[:, g * 2 * WIDE : (g + 1) * 2 * WIDE, :].reshape(depth, BEAMS)
            product = jnp.dot(lhs, weights, preferred_element_type=f32)
            beams.append(product.T)
        for pair in range(together // 2):
            where = (batch * together // 2 + pair) * 16
            for i, b in enumerate(leading(GRP_LEAD, out_ref.shape[0])):
                out_ref[i, where : where + 16, :] = jnp.concatenate(
                    [beams[2 * pair + d][8 * b : 8 * b + 8] for d in range(2)], 0
                ).astype(bf16)


def beamform(spectra, weights, spread):
    stations = weights.shape[0]
    groups = LANES // WIDE
    vmem = pl.BlockSpec(memory_space=pltpu.VMEM)
    return pl.pallas_call(
        beam_kernel,
        out_shape=jax.ShapeDtypeStruct((BEAMS // 8, 8 * groups, LANES), jnp.bfloat16),
        in_specs=[vmem] * 3,
        out_specs=vmem,
        scratch_shapes=[pltpu.VMEM((stations * PARTS, LANES), jnp.float32)],
        compiler_params=pltpu.CompilerParams(vmem_limit_bytes=20 * 2**20),
        name="beamform",
    )(spectra, weights, spread)


def sum_kernel(x_ref, out_ref):
    f32 = jnp.float32
    groups = LANES // WIDE
    held = []
    for g in range(0, groups, 2):
        total = x_ref[0, 8 * g : 8 * g + 16, :].astype(f32)
        for source in range(1, x_ref.shape[0]):
            total = total + x_ref[source, 8 * g : 8 * g + 16, :].astype(f32)
        held += [total[:8], total[8:]]
    block = lax.broadcasted_iota(jnp.int32, (8, LANES), 1) // WIDE
    radix = 4
    for unit in (1, radix):
        digit = block // unit % radix
        turned = [None] * groups
        for i in range(groups):
            mine = i // unit % radix
            total = held[i]
            for other in range(radix):
                if other != mine:
                    moved = pltpu.roll(
                        held[i + (other - mine) * unit], (other - mine) * unit * WIDE % LANES, 1
                    )
                    total = jnp.where(digit == other, moved, total)
            turned[i] = total
        held = turned
    for i in range(groups):
        r, p, s = i // (POLS * SPECTRA), i // SPECTRA % POLS, i % SPECTRA
        out_ref[:, r, p, s, :] = held[i]


def total(parts):
    vmem = pl.BlockSpec(memory_space=pltpu.VMEM)
    return pl.pallas_call(
        sum_kernel,
        out_shape=jax.ShapeDtypeStruct((8, 2, POLS, SPECTRA, LANES), jnp.float32),
        in_specs=[vmem],
        out_specs=vmem,
        compiler_params=pltpu.CompilerParams(vmem_limit_bytes=20 * 2**20),
        name="sum_groups",
    )(parts)


def exchange(blocks, axis, first):
    order = leading(first, blocks.shape[0])
    return lax.all_to_all(
        blocks, axis, split_axis=0, concat_axis=0, axis_index_groups=[order], tiled=True
    )


def shards(voltages, beam_weights, owner_table, live_stations):
    spectra, weights, spread = channelize(voltages, owner_table, live_stations, beam_weights)
    turned = exchange(spectra, "chan", CHAN_LEAD)
    partial = beamform(turned, weights, spread)
    gathered = exchange(partial, "grp", GRP_LEAD)
    return total(gathered)


def solution(mesh):
    in_specs = (
        P(("grp", "chan"), None, None, None),
        P("grp", "chan", None, None),
        P(),
        P(("grp", "chan")),
    )
    out_specs = P("grp", None, None, None, "chan")
    return jax.shard_map(shards, mesh=mesh, in_specs=in_specs, out_specs=out_specs, check_vma=False)
```

```python
import functools

import jax
import jax.numpy as jnp
import numpy as np
from jax import lax
from jax.experimental import pallas as pl
from jax.experimental.pallas import tpu as pltpu
from jax.sharding import PartitionSpec as P

CHANNELS = 4096
TAPS = 16
BEAMS = 128
POLS = 2
SPECTRA = 4
FRAMES = SPECTRA + TAPS - 1
LANES = 128
FIRST = CHANNELS // LANES
ROWS = 2 * FIRST
PARTS = 2 * POLS * SPECTRA
HALF = FIRST // 2
WIDE = 8
CHAN_LEAD = 30
GRP_LEAD = 10


def leading(first, count):
    return [first] + [i for i in range(count) if i != first]


def tap_rows():
    total = TAPS * CHANNELS
    place = np.arange(total, dtype=np.float64)
    window = 0.54 - 0.46 * np.cos(2.0 * np.pi * place / total)
    taps = window * np.sinc((place - total // 2) / CHANNELS) / np.sqrt(CHANNELS)
    taps = taps.reshape(TAPS, FIRST, 1, LANES)
    return np.broadcast_to(taps, (TAPS, FIRST, 2, LANES)).reshape(TAPS, ROWS, LANES)


def first_matrix():
    k, q = np.arange(FIRST)[:, None], np.arange(FIRST)[None, :]
    angle = 2.0 * np.pi * (k * q % FIRST) / FIRST
    cosine, sine = np.cos(angle), np.sin(angle)
    real = np.stack([cosine, sine], 2).reshape(FIRST, ROWS)
    imag = np.stack([-sine, cosine], 2).reshape(FIRST, ROWS)
    whole = np.concatenate([real, imag], 0)
    high = whole.astype(jnp.bfloat16)
    low = (whole - high.astype(np.float64)).astype(jnp.bfloat16)
    return np.concatenate([high, low], 1)


def twiddles():
    k, n = np.arange(FIRST)[:, None], np.arange(LANES)[None, :]
    angle = 2.0 * np.pi * (k * n) / CHANNELS
    return np.stack([np.cos(angle), np.sin(angle)], 0).astype(np.float32)


def second_matrix():
    n, m = np.arange(LANES)[:, None], np.arange(LANES)[None, :]
    angle = 2.0 * np.pi * (n * m % LANES) / LANES
    cosine, sine = np.cos(angle), np.sin(angle)
    return np.block([[cosine, -sine], [sine, cosine]]).astype(jnp.bfloat16)


def spread_matrix(stations):
    out = np.zeros((POLS, 2, stations, 2, POLS, stations, WIDE, 2), np.float32)
    for p in range(POLS):
        for i, st in enumerate(leading(CHAN_LEAD, stations)):
            out[p, 0, i, 0, p, st, :, 0] = 1.0
            out[p, 1, i, 0, p, st, :, 1] = -1.0
            out[p, 1, i, 1, p, st, :, 0] = 1.0
            out[p, 0, i, 1, p, st, :, 1] = 1.0
    return out.reshape(POLS * 2 * stations, 4 * stations * WIDE * 2).astype(jnp.bfloat16)


def channel_kernel(
    v_hbm,
    owner_hbm,
    live_ref,
    taps_hbm,
    matrix_hbm,
    w_hbm,
    spread_hbm,
    out_ref,
    w_ref,
    spread_ref,
    v_ref,
    owner_ref,
    taps_ref,
    matrix_ref,
    pick_ref,
    folded_ref,
    sem,
):
    f32, bf16 = jnp.float32, jnp.bfloat16
    pairs = [
        (owner_hbm, owner_ref),
        (taps_hbm, taps_ref),
        (v_hbm, v_ref),
        (matrix_hbm, matrix_ref),
        (spread_hbm, spread_ref),
        (w_hbm, w_ref),
    ]
    copies = [pltpu.make_async_copy(a, b, sem.at[i]) for i, (a, b) in enumerate(pairs)]
    for copy in copies:
        copy.start()
    blocks = out_ref.shape[0]
    count = POLS * SPECTRA

    copies[0].wait()
    rows = lax.broadcasted_iota(jnp.int32, (2 * LANES, LANES), 0).astype(f32).astype(bf16)
    one, zero = jnp.ones((), bf16), jnp.zeros((), bf16)
    for c in range(blocks):
        owner = owner_ref[c : c + 1, :]
        key = (((owner >> 4) & 1) * LANES + (owner >> 5)).astype(f32).astype(bf16)
        pick_ref[:, c * LANES : (c + 1) * LANES] = jnp.where(rows == key, one, zero)

    copies[1].wait()
    copies[2].wait()
    step = 16
    filtered = [[None] * (ROWS // step) for _ in range(count)]
    for p in range(POLS):
        for c in range(ROWS // step):
            sums = [None] * SPECTRA
            for u in range(FRAMES):
                x = v_ref[p, u * ROWS + c * step : u * ROWS + (c + 1) * step, :].astype(f32)
                for s in range(SPECTRA):
                    t = u - s
                    if 0 <= t < TAPS:
                        term = x * taps_ref[t, c * step : (c + 1) * step, :]
                        sums[s] = term if sums[s] is None else sums[s] + term
            for s in range(SPECTRA):
                filtered[p * SPECTRA + s][c] = sums[s].astype(bf16)
    columns = jnp.concatenate([jnp.concatenate(rows, 0) for rows in filtered], 1)
    copies[3].wait()
    first = jnp.dot(
        matrix_ref[:ROWS], jnp.concatenate([columns, columns], 0), preferred_element_type=f32
    )
    cosine, sine = taps_ref[TAPS, :FIRST], taps_ref[TAPS, FIRST:]
    for i in range(count):
        real = first[:FIRST, i * LANES : (i + 1) * LANES]
        imag = first[FIRST:, i * LANES : (i + 1) * LANES]
        folded_ref[0, pl.ds(i, FIRST, stride=count), :] = real * cosine + imag * sine
        folded_ref[1, pl.ds(i, FIRST, stride=count), :] = imag * cosine - real * sine
    folded = jnp.concatenate([folded_ref[0], folded_ref[1]], 1).astype(bf16)
    second = jnp.concatenate([matrix_ref[ROWS : 5 * LANES // 2], matrix_ref[5 * LANES // 2 :]], 1)
    spectrum = jnp.dot(folded, second, preferred_element_type=f32)
    spectrum = spectrum.astype(bf16).astype(f32) * live_ref[0].astype(f32)
    cut = HALF * count
    table = jnp.concatenate(
        [
            jnp.concatenate([spectrum[:cut, :LANES], spectrum[cut:, :LANES]], 1),
            jnp.concatenate([spectrum[:cut, LANES:], spectrum[cut:, LANES:]], 1),
        ],
        0,
    ).astype(bf16)
    place_of = {c: i for i, c in enumerate(leading(CHAN_LEAD, blocks))}
    for c in range(0, blocks, 2):
        found = jnp.dot(
            table, pick_ref[:, c * LANES : (c + 2) * LANES], preferred_element_type=f32
        )
        for d in range(2):
            low = jnp.broadcast_to(owner_ref[c + d : c + d + 1, :] & 15, (count, LANES))
            parts = []
            for r in range(2):
                block = found[r * cut : (r + 1) * cut, d * LANES : (d + 1) * LANES]
                total = block[:count]
                for h in range(1, HALF):
                    total = jnp.where(low == h, block[h * count : (h + 1) * count], total)
                parts.append(total)
            out_ref[place_of[c + d]] = jnp.concatenate(parts, 0).astype(bf16)
    copies[4].wait()
    copies[5].wait()


def place(array):
    return pltpu.with_memory_space_constraint(array, pltpu.HBM)


def channelize(volts, owner_table, live, weights):
    volts = volts.reshape(POLS, 2, FRAMES * FIRST, LANES)
    volts = jnp.transpose(volts, (0, 2, 1, 3)).reshape(POLS, FRAMES * ROWS, LANES)
    owner = owner_table.reshape(CHANNELS // LANES, LANES)
    stations = weights.shape[0]
    weights = weights.reshape(stations, LANES * 2, BEAMS)
    second = second_matrix()
    constants = [
        jnp.asarray(np.concatenate([tap_rows(), twiddles().reshape(1, ROWS, LANES)]), jnp.float32),
        jnp.asarray(np.concatenate([first_matrix(), second[:, :LANES], second[:, LANES:]])),
    ]
    spread = jnp.asarray(spread_matrix(stations))
    vmem = pl.BlockSpec(memory_space=pltpu.VMEM)
    hbm = pl.BlockSpec(memory_space=pltpu.HBM)
    held = [pltpu.VMEM(a.shape, a.dtype) for a in [volts, owner] + constants]
    return pl.pallas_call(
        channel_kernel,
        out_shape=[
            jax.ShapeDtypeStruct((CHANNELS // LANES, PARTS, LANES), jnp.bfloat16),
            jax.ShapeDtypeStruct(weights.shape, jnp.bfloat16),
            jax.ShapeDtypeStruct(spread.shape, jnp.bfloat16),
        ],
        in_specs=[hbm, hbm, pl.BlockSpec(memory_space=pltpu.SMEM)] + [hbm] * 4,
        out_specs=[vmem] * 3,
        scratch_shapes=held
        + [
            pltpu.VMEM((2 * LANES, CHANNELS), jnp.bfloat16),
            pltpu.VMEM((2, FIRST * POLS * SPECTRA, LANES), jnp.float32),
            pltpu.SemaphoreType.DMA((6,)),
        ],
        compiler_params=pltpu.CompilerParams(vmem_limit_bytes=20 * 2**20),
        name="channelize",
    )(*[place(a) for a in (volts, owner)], live, *[place(a) for a in constants + [weights, spread]])


def beam_kernel(x_ref, w_ref, spread_ref, out_ref, wide_ref):
    f32, bf16 = jnp.float32, jnp.bfloat16
    stations = x_ref.shape[0]
    groups = LANES // WIDE
    wide_ref[...] = x_ref[...].reshape(stations * PARTS, LANES).astype(f32)
    turned = []
    for s in range(SPECTRA):
        rows = []
        for p in range(POLS):
            for r in range(2):
                start = r * POLS * SPECTRA + p * SPECTRA + s
                rows.append(wide_ref[pl.ds(start, stations, stride=PARTS), :])
        turned.append(jnp.concatenate(rows, 0).T)
    depth = stations * WIDE * 2
    row_slot = lax.broadcasted_iota(jnp.int32, (SPECTRA * WIDE, depth), 0) % WIDE
    column_slot = lax.broadcasted_iota(jnp.int32, (SPECTRA * WIDE, depth), 1) // 2 % WIDE
    meets = row_slot == column_slot
    together = 16
    height = SPECTRA * WIDE
    for batch in range(groups // together):
        small = []
        for g in range(batch * together, (batch + 1) * together):
            for s in range(SPECTRA):
                small.append(turned[s][g * WIDE : (g + 1) * WIDE])
        spread = jnp.dot(
            jnp.concatenate(small, 0).astype(bf16), spread_ref[...], preferred_element_type=f32
        )
        beams = []
        for i in range(together):
            g = batch * together + i
            lhs = jnp.concatenate(
                [
                    jnp.where(
                        meets,
                        spread[i * height : (i + 1) * height, b * depth : (b + 1) * depth],
                        0.0,
                    ).astype(bf16)
                    for b in range(2 * POLS)
                ],
                0,
            )
            weights = w_ref[:, g * 2 * WIDE : (g + 1) * 2 * WIDE, :].reshape(depth, BEAMS)
            product = jnp.dot(lhs, weights, preferred_element_type=f32)
            beams.append(product.T)
        for pair in range(together // 2):
            where = (batch * together // 2 + pair) * 16
            for i, b in enumerate(leading(GRP_LEAD, out_ref.shape[0])):
                out_ref[i, where : where + 16, :] = jnp.concatenate(
                    [beams[2 * pair + d][8 * b : 8 * b + 8] for d in range(2)], 0
                ).astype(bf16)


def beamform(spectra, weights, spread):
    stations = weights.shape[0]
    groups = LANES // WIDE
    vmem = pl.BlockSpec(memory_space=pltpu.VMEM)
    return pl.pallas_call(
        beam_kernel,
        out_shape=jax.ShapeDtypeStruct((BEAMS // 8, 8 * groups, LANES), jnp.bfloat16),
        in_specs=[vmem] * 3,
        out_specs=vmem,
        scratch_shapes=[pltpu.VMEM((stations * PARTS, LANES), jnp.float32)],
        compiler_params=pltpu.CompilerParams(vmem_limit_bytes=20 * 2**20),
        name="beamform",
    )(spectra, weights, spread)


def sum_kernel(x_ref, out_ref):
    f32 = jnp.float32
    groups = LANES // WIDE
    held = []
    for g in range(0, groups, 2):
        total = x_ref[0, 8 * g : 8 * g + 16, :].astype(f32)
        for source in range(1, x_ref.shape[0]):
            total = total + x_ref[source, 8 * g : 8 * g + 16, :].astype(f32)
        held += [total[:8], total[8:]]
    block = lax.broadcasted_iota(jnp.int32, (8, LANES), 1) // WIDE
    radix = 4
    for unit in (1, radix):
        digit = block // unit % radix
        turned = [None] * groups
        for i in range(groups):
            mine = i // unit % radix
            total = held[i]
            for other in range(radix):
                if other != mine:
                    moved = pltpu.roll(
                        held[i + (other - mine) * unit], (other - mine) * unit * WIDE % LANES, 1
                    )
                    total = jnp.where(digit == other, moved, total)
            turned[i] = total
        held = turned
    for i in range(groups):
        r, p, s = i // (POLS * SPECTRA), i // SPECTRA % POLS, i % SPECTRA
        out_ref[:, r, p, s, :] = held[i]


def total(parts):
    vmem = pl.BlockSpec(memory_space=pltpu.VMEM)
    return pl.pallas_call(
        sum_kernel,
        out_shape=jax.ShapeDtypeStruct((8, 2, POLS, SPECTRA, LANES), jnp.float32),
        in_specs=[vmem],
        out_specs=vmem,
        compiler_params=pltpu.CompilerParams(vmem_limit_bytes=20 * 2**20),
        name="sum_groups",
    )(parts)


def exchange(blocks, axis, first):
    order = leading(first, blocks.shape[0])
    return lax.all_to_all(
        blocks, axis, split_axis=0, concat_axis=0, axis_index_groups=[order], tiled=True
    )


def shards(voltages, beam_weights, owner_table, live_stations):
    spectra, weights, spread = channelize(voltages, owner_table, live_stations, beam_weights)
    turned = exchange(spectra, "chan", CHAN_LEAD)
    partial = beamform(turned, weights, spread)
    gathered = exchange(partial, "grp", GRP_LEAD)
    return total(gathered)


def solution(mesh):
    in_specs = (
        P(("grp", "chan"), None, None, None),
        P("grp", "chan", None, None),
        P(),
        P(("grp", "chan")),
    )
    out_specs = P("grp", None, None, None, "chan")
    return jax.shard_map(shards, mesh=mesh, in_specs=in_specs, out_specs=out_specs, check_vma=False)
```

```python
import functools

import jax
import jax.numpy as jnp
import numpy as np
from jax import lax
from jax.experimental import pallas as pl
from jax.experimental.pallas import tpu as pltpu
from jax.sharding import PartitionSpec as P

CHANNELS = 4096
TAPS = 16
BEAMS = 128
POLS = 2
SPECTRA = 4
FRAMES = SPECTRA + TAPS - 1
LANES = 128
FIRST = CHANNELS // LANES
ROWS = 2 * FIRST
PARTS = 2 * POLS * SPECTRA
HALF = FIRST // 2
WIDE = 8
CHAN_LEAD = 30
GRP_LEAD = 10


def leading(first, count):
    return [first] + [i for i in range(count) if i != first]


def tap_rows():
    total = TAPS * CHANNELS
    place = np.arange(total, dtype=np.float64)
    window = 0.54 - 0.46 * np.cos(2.0 * np.pi * place / total)
    taps = window * np.sinc((place - total // 2) / CHANNELS) / np.sqrt(CHANNELS)
    taps = taps.reshape(TAPS, FIRST, 1, LANES)
    return np.broadcast_to(taps, (TAPS, FIRST, 2, LANES)).reshape(TAPS, ROWS, LANES)


def first_matrix():
    k, q = np.arange(FIRST)[:, None], np.arange(FIRST)[None, :]
    angle = 2.0 * np.pi * (k * q % FIRST) / FIRST
    cosine, sine = np.cos(angle), np.sin(angle)
    real = np.stack([cosine, sine], 2).reshape(FIRST, ROWS)
    imag = np.stack([-sine, cosine], 2).reshape(FIRST, ROWS)
    whole = np.concatenate([real, imag], 0)
    high = whole.astype(jnp.bfloat16)
    low = (whole - high.astype(np.float64)).astype(jnp.bfloat16)
    return np.concatenate([high, low], 1)


def twiddles():
    k, n = np.arange(FIRST)[:, None], np.arange(LANES)[None, :]
    angle = 2.0 * np.pi * (k * n) / CHANNELS
    return np.stack([np.cos(angle), np.sin(angle)], 0).astype(np.float32)


def second_matrix():
    n, m = np.arange(LANES)[:, None], np.arange(LANES)[None, :]
    angle = 2.0 * np.pi * (n * m % LANES) / LANES
    cosine, sine = np.cos(angle), np.sin(angle)
    return np.block([[cosine, -sine], [sine, cosine]]).astype(jnp.bfloat16)


def spread_matrix(stations):
    out = np.zeros((POLS, 2, stations, POLS, stations, WIDE, 2), np.float32)
    for p in range(POLS):
        for i, st in enumerate(leading(CHAN_LEAD, stations)):
            out[p, 0, i, p, st, :, 0] = 1.0
            out[p, 1, i, p, st, :, 1] = -1.0
    return out.reshape(POLS * 2 * stations, POLS * stations * WIDE * 2).astype(jnp.bfloat16)


def channel_kernel(
    v_hbm,
    owner_hbm,
    live_ref,
    taps_hbm,
    matrix_hbm,
    w_hbm,
    spread_hbm,
    out_ref,
    w_ref,
    spread_ref,
    v_ref,
    owner_ref,
    taps_ref,
    matrix_ref,
    pick_ref,
    folded_ref,
    sem,
):
    f32, bf16 = jnp.float32, jnp.bfloat16
    pairs = [
        (owner_hbm, owner_ref),
        (taps_hbm, taps_ref),
        (v_hbm, v_ref),
        (matrix_hbm, matrix_ref),
        (spread_hbm, spread_ref),
        (w_hbm, w_ref),
    ]
    copies = [pltpu.make_async_copy(a, b, sem.at[i]) for i, (a, b) in enumerate(pairs)]
    for copy in copies:
        copy.start()
    blocks = out_ref.shape[0]
    count = POLS * SPECTRA

    copies[0].wait()
    rows = lax.broadcasted_iota(jnp.int32, (2 * LANES, LANES), 0).astype(f32).astype(bf16)
    one, zero = jnp.ones((), bf16), jnp.zeros((), bf16)
    for c in range(blocks):
        owner = owner_ref[c : c + 1, :]
        key = (((owner >> 4) & 1) * LANES + (owner >> 5)).astype(f32).astype(bf16)
        pick_ref[:, c * LANES : (c + 1) * LANES] = jnp.where(rows == key, one, zero)

    copies[1].wait()
    copies[2].wait()
    step = 16
    filtered = [[None] * (ROWS // step) for _ in range(count)]
    for p in range(POLS):
        for c in range(ROWS // step):
            sums = [None] * SPECTRA
            for u in range(FRAMES):
                x = v_ref[p, u * ROWS + c * step : u * ROWS + (c + 1) * step, :].astype(f32)
                for s in range(SPECTRA):
                    t = u - s
                    if 0 <= t < TAPS:
                        term = x * taps_ref[t, c * step : (c + 1) * step, :]
                        sums[s] = term if sums[s] is None else sums[s] + term
            for s in range(SPECTRA):
                filtered[p * SPECTRA + s][c] = sums[s].astype(bf16)
    columns = jnp.concatenate([jnp.concatenate(rows, 0) for rows in filtered], 1)
    copies[3].wait()
    first = jnp.dot(
        matrix_ref[:ROWS], jnp.concatenate([columns, columns], 0), preferred_element_type=f32
    )
    cosine, sine = taps_ref[TAPS, :FIRST], taps_ref[TAPS, FIRST:]
    for i in range(count):
        real = first[:FIRST, i * LANES : (i + 1) * LANES]
        imag = first[FIRST:, i * LANES : (i + 1) * LANES]
        folded_ref[0, pl.ds(i, FIRST, stride=count), :] = real * cosine + imag * sine
        folded_ref[1, pl.ds(i, FIRST, stride=count), :] = imag * cosine - real * sine
    folded = jnp.concatenate([folded_ref[0], folded_ref[1]], 1).astype(bf16)
    second = jnp.concatenate([matrix_ref[ROWS : 5 * LANES // 2], matrix_ref[5 * LANES // 2 :]], 1)
    spectrum = jnp.dot(folded, second, preferred_element_type=f32)
    spectrum = spectrum.astype(bf16).astype(f32) * live_ref[0].astype(f32)
    cut = HALF * count
    table = jnp.concatenate(
        [
            jnp.concatenate([spectrum[:cut, :LANES], spectrum[cut:, :LANES]], 1),
            jnp.concatenate([spectrum[:cut, LANES:], spectrum[cut:, LANES:]], 1),
        ],
        0,
    ).astype(bf16)
    place_of = {c: i for i, c in enumerate(leading(CHAN_LEAD, blocks))}
    for c in range(0, blocks, 2):
        found = jnp.dot(
            table, pick_ref[:, c * LANES : (c + 2) * LANES], preferred_element_type=f32
        )
        for d in range(2):
            low = jnp.broadcast_to(owner_ref[c + d : c + d + 1, :] & 15, (count, LANES))
            parts = []
            for r in range(2):
                block = found[r * cut : (r + 1) * cut, d * LANES : (d + 1) * LANES]
                total = block[:count]
                for h in range(1, HALF):
                    total = jnp.where(low == h, block[h * count : (h + 1) * count], total)
                parts.append(total)
            out_ref[place_of[c + d]] = jnp.concatenate(parts, 0).astype(bf16)
    copies[4].wait()
    copies[5].wait()


def place(array):
    return pltpu.with_memory_space_constraint(array, pltpu.HBM)


def channelize(volts, owner_table, live, weights):
    volts = volts.reshape(POLS, 2, FRAMES * FIRST, LANES)
    volts = jnp.transpose(volts, (0, 2, 1, 3)).reshape(POLS, FRAMES * ROWS, LANES)
    owner = owner_table.reshape(CHANNELS // LANES, LANES)
    stations = weights.shape[0]
    weights = weights.reshape(stations, LANES * 2, BEAMS)
    second = second_matrix()
    constants = [
        jnp.asarray(np.concatenate([tap_rows(), twiddles().reshape(1, ROWS, LANES)]), jnp.float32),
        jnp.asarray(np.concatenate([first_matrix(), second[:, :LANES], second[:, LANES:]])),
    ]
    spread = jnp.asarray(spread_matrix(stations))
    vmem = pl.BlockSpec(memory_space=pltpu.VMEM)
    hbm = pl.BlockSpec(memory_space=pltpu.HBM)
    held = [pltpu.VMEM(a.shape, a.dtype) for a in [volts, owner] + constants]
    return pl.pallas_call(
        channel_kernel,
        out_shape=[
            jax.ShapeDtypeStruct((CHANNELS // LANES, PARTS, LANES), jnp.bfloat16),
            jax.ShapeDtypeStruct(weights.shape, jnp.bfloat16),
            jax.ShapeDtypeStruct(spread.shape, jnp.bfloat16),
        ],
        in_specs=[hbm, hbm, pl.BlockSpec(memory_space=pltpu.SMEM)] + [hbm] * 4,
        out_specs=[vmem] * 3,
        scratch_shapes=held
        + [
            pltpu.VMEM((2 * LANES, CHANNELS), jnp.bfloat16),
            pltpu.VMEM((2, FIRST * POLS * SPECTRA, LANES), jnp.float32),
            pltpu.SemaphoreType.DMA((6,)),
        ],
        compiler_params=pltpu.CompilerParams(vmem_limit_bytes=20 * 2**20),
        name="channelize",
    )(*[place(a) for a in (volts, owner)], live, *[place(a) for a in constants + [weights, spread]])


def beam_kernel(x_ref, w_ref, spread_ref, out_ref, wide_ref):
    f32, bf16 = jnp.float32, jnp.bfloat16
    stations = x_ref.shape[0]
    groups = LANES // WIDE
    wide_ref[...] = x_ref[...].reshape(stations * PARTS, LANES).astype(f32)
    turned = []
    for s in range(SPECTRA):
        rows = []
        for p in range(POLS):
            for r in range(2):
                start = r * POLS * SPECTRA + p * SPECTRA + s
                rows.append(wide_ref[pl.ds(start, stations, stride=PARTS), :])
        turned.append(jnp.concatenate(rows, 0).T)
    depth = stations * WIDE * 2
    height = SPECTRA * WIDE
    row_slot = lax.broadcasted_iota(jnp.int32, (height, depth), 0) % WIDE
    column_slot = lax.broadcasted_iota(jnp.int32, (height, depth), 1) // 2 % WIDE
    meets = row_slot == column_slot
    by_product = POLS
    small = []
    for g in range(groups):
        for s in range(SPECTRA):
            small.append(turned[s][g * WIDE : (g + 1) * WIDE])
    spread = jnp.dot(
        jnp.concatenate(small, 0).astype(bf16),
        spread_ref[...],
        preferred_element_type=f32,
    )
    lane = lax.broadcasted_iota(jnp.int32, (LANES, LANES), 1)
    held = LANES // (2 * WIDE)
    moved = {}
    for b in range(by_product, 2 * POLS):
        p = b % POLS
        for c in range(depth // LANES):
            station = c * held + lane // (2 * WIDE)
            at = jnp.where(station < CHAN_LEAD, station + 1, station)
            at = jnp.where(station == CHAN_LEAD, 0, at)
            index = (p * 2 + 1 - lane % 2) * stations + at
            for s in range(SPECTRA):
                moved[b, c, s] = jnp.take_along_axis(turned[s], index, axis=1)
    beams = []
    for g in range(groups):
        here = slice(g * WIDE, (g + 1) * WIDE)
        blocks = []
        for b in range(2 * POLS):
            if b < by_product:
                block = spread[g * height : (g + 1) * height, b * depth : (b + 1) * depth]
            else:
                block = jnp.concatenate(
                    [
                        jnp.concatenate([moved[b, c, s][here] for s in range(SPECTRA)], 0)
                        for c in range(depth // LANES)
                    ],
                    1,
                )
            blocks.append(jnp.where(meets, block, 0.0).astype(bf16))
        weights = w_ref[:, g * 2 * WIDE : (g + 1) * 2 * WIDE, :].reshape(depth, BEAMS)
        product = jnp.dot(jnp.concatenate(blocks, 0), weights, preferred_element_type=f32)
        beams.append(product.T)
        if g % 2:
            where = g // 2 * 16
            for i, b in enumerate(leading(GRP_LEAD, out_ref.shape[0])):
                out_ref[i, where : where + 16, :] = jnp.concatenate(
                    [beams[g - 1 + d][8 * b : 8 * b + 8] for d in range(2)], 0
                ).astype(bf16)


def beamform(spectra, weights, spread):
    stations = weights.shape[0]
    groups = LANES // WIDE
    vmem = pl.BlockSpec(memory_space=pltpu.VMEM)
    return pl.pallas_call(
        beam_kernel,
        out_shape=jax.ShapeDtypeStruct((BEAMS // 8, 8 * groups, LANES), jnp.bfloat16),
        in_specs=[vmem] * 3,
        out_specs=vmem,
        scratch_shapes=[pltpu.VMEM((stations * PARTS, LANES), jnp.float32)],
        compiler_params=pltpu.CompilerParams(vmem_limit_bytes=20 * 2**20),
        name="beamform",
    )(spectra, weights, spread)


def sum_kernel(x_ref, out_ref):
    f32 = jnp.float32
    groups = LANES // WIDE
    held = []
    for g in range(0, groups, 2):
        total = x_ref[0, 8 * g : 8 * g + 16, :].astype(f32)
        for source in range(1, x_ref.shape[0]):
            total = total + x_ref[source, 8 * g : 8 * g + 16, :].astype(f32)
        held += [total[:8], total[8:]]
    block = lax.broadcasted_iota(jnp.int32, (8, LANES), 1) // WIDE
    radix = 4
    for unit in (1, radix):
        digit = block // unit % radix
        turned = [None] * groups
        for i in range(groups):
            mine = i // unit % radix
            total = held[i]
            for other in range(radix):
                if other != mine:
                    moved = pltpu.roll(
                        held[i + (other - mine) * unit], (other - mine) * unit * WIDE % LANES, 1
                    )
                    total = jnp.where(digit == other, moved, total)
            turned[i] = total
        held = turned
    for i in range(groups):
        r, p, s = i // (POLS * SPECTRA), i // SPECTRA % POLS, i % SPECTRA
        out_ref[:, r, p, s, :] = held[i]


def total(parts):
    vmem = pl.BlockSpec(memory_space=pltpu.VMEM)
    return pl.pallas_call(
        sum_kernel,
        out_shape=jax.ShapeDtypeStruct((8, 2, POLS, SPECTRA, LANES), jnp.float32),
        in_specs=[vmem],
        out_specs=vmem,
        compiler_params=pltpu.CompilerParams(vmem_limit_bytes=20 * 2**20),
        name="sum_groups",
    )(parts)


def exchange(blocks, axis, first):
    order = leading(first, blocks.shape[0])
    return lax.all_to_all(
        blocks, axis, split_axis=0, concat_axis=0, axis_index_groups=[order], tiled=True
    )


def shards(voltages, beam_weights, owner_table, live_stations):
    spectra, weights, spread = channelize(voltages, owner_table, live_stations, beam_weights)
    turned = exchange(spectra, "chan", CHAN_LEAD)
    partial = beamform(turned, weights, spread)
    gathered = exchange(partial, "grp", GRP_LEAD)
    return total(gathered)


def solution(mesh):
    in_specs = (
        P(("grp", "chan"), None, None, None),
        P("grp", "chan", None, None),
        P(),
        P(("grp", "chan")),
    )
    out_specs = P("grp", None, None, None, "chan")
    return jax.shard_map(shards, mesh=mesh, in_specs=in_specs, out_specs=out_specs, check_vma=False)
```

```python
import functools

import jax
import jax.numpy as jnp
import numpy as np
from jax import lax
from jax.experimental import pallas as pl
from jax.experimental.pallas import tpu as pltpu
from jax.sharding import PartitionSpec as P

CHANNELS = 4096
TAPS = 16
BEAMS = 128
POLS = 2
SPECTRA = 4
FRAMES = SPECTRA + TAPS - 1
LANES = 128
FIRST = CHANNELS // LANES
ROWS = 2 * FIRST
PARTS = 2 * POLS * SPECTRA
HALF = FIRST // 2
WIDE = 8
CHAN_LEAD = 30
GRP_LEAD = 10


def leading(first, count):
    return [first] + [i for i in range(count) if i != first]


def tap_rows():
    total = TAPS * CHANNELS
    place = np.arange(total, dtype=np.float64)
    window = 0.54 - 0.46 * np.cos(2.0 * np.pi * place / total)
    taps = window * np.sinc((place - total // 2) / CHANNELS) / np.sqrt(CHANNELS)
    taps = taps.reshape(TAPS, FIRST, 1, LANES)
    return np.broadcast_to(taps, (TAPS, FIRST, 2, LANES)).reshape(TAPS, ROWS, LANES)


def first_matrix():
    k, q = np.arange(FIRST)[:, None], np.arange(FIRST)[None, :]
    angle = 2.0 * np.pi * (k * q % FIRST) / FIRST
    cosine, sine = np.cos(angle), np.sin(angle)
    real = np.stack([cosine, sine], 2).reshape(FIRST, ROWS)
    imag = np.stack([-sine, cosine], 2).reshape(FIRST, ROWS)
    whole = np.concatenate([real, imag], 0)
    high = whole.astype(jnp.bfloat16)
    low = (whole - high.astype(np.float64)).astype(jnp.bfloat16)
    return np.concatenate([high, low], 1)


def twiddles():
    k, n = np.arange(FIRST)[:, None], np.arange(LANES)[None, :]
    angle = 2.0 * np.pi * (k * n) / CHANNELS
    return np.stack([np.cos(angle), np.sin(angle)], 0).astype(np.float32)


def second_matrix():
    n, m = np.arange(LANES)[:, None], np.arange(LANES)[None, :]
    angle = 2.0 * np.pi * (n * m % LANES) / LANES
    cosine, sine = np.cos(angle), np.sin(angle)
    return np.block([[cosine, -sine], [sine, cosine]]).astype(jnp.bfloat16)


def spread_matrix(stations):
    out = np.zeros((POLS, 2, stations, POLS, stations, WIDE, 2), np.float32)
    for p in range(POLS):
        for i, st in enumerate(leading(CHAN_LEAD, stations)):
            out[p, 0, i, p, st, :, 0] = 1.0
            out[p, 1, i, p, st, :, 1] = -1.0
    return out.reshape(POLS * 2 * stations, POLS * stations * WIDE * 2).astype(jnp.bfloat16)


def channel_kernel(
    v_hbm,
    owner_hbm,
    live_ref,
    taps_hbm,
    matrix_hbm,
    w_hbm,
    spread_hbm,
    out_ref,
    w_ref,
    spread_ref,
    v_ref,
    owner_ref,
    taps_ref,
    matrix_ref,
    pick_ref,
    sem,
):
    f32, bf16 = jnp.float32, jnp.bfloat16
    pairs = [
        (owner_hbm, owner_ref),
        (taps_hbm, taps_ref),
        (v_hbm, v_ref),
        (matrix_hbm, matrix_ref),
        (spread_hbm, spread_ref),
        (w_hbm, w_ref),
    ]
    copies = [pltpu.make_async_copy(a, b, sem.at[i]) for i, (a, b) in enumerate(pairs)]
    for copy in copies:
        copy.start()
    blocks = out_ref.shape[0]
    count = POLS * SPECTRA

    copies[0].wait()
    rows = lax.broadcasted_iota(jnp.int32, (2 * LANES, LANES), 0).astype(f32).astype(bf16)
    one, zero = jnp.ones((), bf16), jnp.zeros((), bf16)
    for c in range(blocks):
        owner = owner_ref[c : c + 1, :]
        key = (((owner >> 4) & 1) * LANES + (owner >> 5)).astype(f32).astype(bf16)
        pick_ref[:, c * LANES : (c + 1) * LANES] = jnp.where(rows == key, one, zero)

    copies[1].wait()
    copies[2].wait()
    step = 16
    filtered = [[None] * (ROWS // step) for _ in range(count)]
    for p in range(POLS):
        for c in range(ROWS // step):
            sums = [None] * SPECTRA
            for u in range(FRAMES):
                x = v_ref[p, u * ROWS + c * step : u * ROWS + (c + 1) * step, :].astype(f32)
                for s in range(SPECTRA):
                    t = u - s
                    if 0 <= t < TAPS:
                        term = x * taps_ref[t, c * step : (c + 1) * step, :]
                        sums[s] = term if sums[s] is None else sums[s] + term
            for s in range(SPECTRA):
                filtered[p * SPECTRA + s][c] = sums[s].astype(bf16)
    columns = jnp.concatenate([jnp.concatenate(rows, 0) for rows in filtered], 1)
    copies[3].wait()
    first = jnp.dot(
        matrix_ref[:ROWS], jnp.concatenate([columns, columns], 0), preferred_element_type=f32
    )
    cosine, sine = taps_ref[TAPS, :FIRST], taps_ref[TAPS, FIRST:]
    halves = [[], []]
    for i in range(count):
        real = first[:FIRST, i * LANES : (i + 1) * LANES]
        imag = first[FIRST:, i * LANES : (i + 1) * LANES]
        halves[0].append(real * cosine + imag * sine)
        halves[1].append(imag * cosine - real * sine)
    folded = jnp.concatenate(
        [jnp.swapaxes(jnp.stack(h, 0), 0, 1).reshape(FIRST * count, LANES) for h in halves], 1
    ).astype(bf16)
    second = jnp.concatenate([matrix_ref[ROWS : 5 * LANES // 2], matrix_ref[5 * LANES // 2 :]], 1)
    spectrum = jnp.dot(folded, second, preferred_element_type=f32)
    spectrum = spectrum.astype(bf16).astype(f32) * live_ref[0].astype(f32)
    cut = HALF * count
    table = jnp.concatenate(
        [
            jnp.concatenate([spectrum[:cut, :LANES], spectrum[cut:, :LANES]], 1),
            jnp.concatenate([spectrum[:cut, LANES:], spectrum[cut:, LANES:]], 1),
        ],
        0,
    ).astype(bf16)
    place_of = {c: i for i, c in enumerate(leading(CHAN_LEAD, blocks))}
    for c in range(0, blocks, 2):
        found = jnp.dot(
            table, pick_ref[:, c * LANES : (c + 2) * LANES], preferred_element_type=f32
        )
        for d in range(2):
            low = jnp.broadcast_to(owner_ref[c + d : c + d + 1, :] & 15, (count, LANES))
            parts = []
            for r in range(2):
                block = found[r * cut : (r + 1) * cut, d * LANES : (d + 1) * LANES]
                total = block[:count]
                for h in range(1, HALF):
                    total = jnp.where(low == h, block[h * count : (h + 1) * count], total)
                parts.append(total)
            out_ref[place_of[c + d]] = jnp.concatenate(parts, 0).astype(bf16)
    copies[4].wait()
    copies[5].wait()


def place(array):
    return pltpu.with_memory_space_constraint(array, pltpu.HBM)


def channelize(volts, owner_table, live, weights):
    volts = volts.reshape(POLS, 2, FRAMES * FIRST, LANES)
    volts = jnp.transpose(volts, (0, 2, 1, 3)).reshape(POLS, FRAMES * ROWS, LANES)
    owner = owner_table.reshape(CHANNELS // LANES, LANES)
    stations = weights.shape[0]
    weights = weights.reshape(stations, LANES * 2, BEAMS)
    second = second_matrix()
    constants = [
        jnp.asarray(np.concatenate([tap_rows(), twiddles().reshape(1, ROWS, LANES)]), jnp.float32),
        jnp.asarray(np.concatenate([first_matrix(), second[:, :LANES], second[:, LANES:]])),
    ]
    spread = jnp.asarray(spread_matrix(stations))
    vmem = pl.BlockSpec(memory_space=pltpu.VMEM)
    hbm = pl.BlockSpec(memory_space=pltpu.HBM)
    held = [pltpu.VMEM(a.shape, a.dtype) for a in [volts, owner] + constants]
    return pl.pallas_call(
        channel_kernel,
        out_shape=[
            jax.ShapeDtypeStruct((CHANNELS // LANES, PARTS, LANES), jnp.bfloat16),
            jax.ShapeDtypeStruct(weights.shape, jnp.bfloat16),
            jax.ShapeDtypeStruct(spread.shape, jnp.bfloat16),
        ],
        in_specs=[hbm, hbm, pl.BlockSpec(memory_space=pltpu.SMEM)] + [hbm] * 4,
        out_specs=[vmem] * 3,
        scratch_shapes=held
        + [
            pltpu.VMEM((2 * LANES, CHANNELS), jnp.bfloat16),
            pltpu.SemaphoreType.DMA((6,)),
        ],
        compiler_params=pltpu.CompilerParams(vmem_limit_bytes=20 * 2**20),
        name="channelize",
    )(*[place(a) for a in (volts, owner)], live, *[place(a) for a in constants + [weights, spread]])


def beam_kernel(x_ref, w_ref, spread_ref, out_ref, wide_ref):
    f32, bf16 = jnp.float32, jnp.bfloat16
    stations = x_ref.shape[0]
    groups = LANES // WIDE
    wide_ref[...] = x_ref[...].reshape(stations * PARTS, LANES).astype(f32)
    turned = []
    for s in range(SPECTRA):
        rows = []
        for p in range(POLS):
            for r in range(2):
                start = r * POLS * SPECTRA + p * SPECTRA + s
                rows.append(wide_ref[pl.ds(start, stations, stride=PARTS), :])
        turned.append(jnp.concatenate(rows, 0).T)
    depth = stations * WIDE * 2
    height = SPECTRA * WIDE
    row_slot = lax.broadcasted_iota(jnp.int32, (height, depth), 0) % WIDE
    column_slot = lax.broadcasted_iota(jnp.int32, (height, depth), 1) // 2 % WIDE
    meets = row_slot == column_slot
    by_product = POLS
    small = []
    for g in range(groups):
        for s in range(SPECTRA):
            small.append(turned[s][g * WIDE : (g + 1) * WIDE])
    spread = jnp.dot(
        jnp.concatenate(small, 0).astype(bf16),
        spread_ref[...],
        preferred_element_type=f32,
    )
    lane = lax.broadcasted_iota(jnp.int32, (LANES, LANES), 1)
    held = LANES // (2 * WIDE)
    moved = {}
    for b in range(by_product, 2 * POLS):
        p = b % POLS
        for c in range(depth // LANES):
            station = c * held + lane // (2 * WIDE)
            at = jnp.where(station < CHAN_LEAD, station + 1, station)
            at = jnp.where(station == CHAN_LEAD, 0, at)
            index = (p * 2 + 1 - lane % 2) * stations + at
            for s in range(SPECTRA):
                moved[b, c, s] = jnp.take_along_axis(turned[s], index, axis=1)
    beams = []
    for g in range(groups):
        here = slice(g * WIDE, (g + 1) * WIDE)
        blocks = []
        for b in range(2 * POLS):
            if b < by_product:
                block = spread[g * height : (g + 1) * height, b * depth : (b + 1) * depth]
            else:
                block = jnp.concatenate(
                    [
                        jnp.concatenate([moved[b, c, s][here] for s in range(SPECTRA)], 0)
                        for c in range(depth // LANES)
                    ],
                    1,
                )
            blocks.append(jnp.where(meets, block, 0.0).astype(bf16))
        weights = w_ref[:, g * 2 * WIDE : (g + 1) * 2 * WIDE, :].reshape(depth, BEAMS)
        product = jnp.dot(jnp.concatenate(blocks, 0), weights, preferred_element_type=f32)
        beams.append(product.astype(bf16).T.astype(f32))
        if g % 2:
            where = g // 2 * 16
            for i, b in enumerate(leading(GRP_LEAD, out_ref.shape[0])):
                out_ref[i, where : where + 16, :] = jnp.concatenate(
                    [beams[g - 1 + d][8 * b : 8 * b + 8] for d in range(2)], 0
                ).astype(bf16)


def beamform(spectra, weights, spread):
    stations = weights.shape[0]
    groups = LANES // WIDE
    vmem = pl.BlockSpec(memory_space=pltpu.VMEM)
    return pl.pallas_call(
        beam_kernel,
        out_shape=jax.ShapeDtypeStruct((BEAMS // 8, 8 * groups, LANES), jnp.bfloat16),
        in_specs=[vmem] * 3,
        out_specs=vmem,
        scratch_shapes=[pltpu.VMEM((stations * PARTS, LANES), jnp.float32)],
        compiler_params=pltpu.CompilerParams(vmem_limit_bytes=20 * 2**20),
        name="beamform",
    )(spectra, weights, spread)


def sum_kernel(x_ref, out_ref):
    f32 = jnp.float32
    groups = LANES // WIDE
    held = []
    for g in range(0, groups, 2):
        total = x_ref[0, 8 * g : 8 * g + 16, :].astype(f32)
        for source in range(1, x_ref.shape[0]):
            total = total + x_ref[source, 8 * g : 8 * g + 16, :].astype(f32)
        held += [total[:8], total[8:]]
    block = lax.broadcasted_iota(jnp.int32, (8, LANES), 1) // WIDE
    radix = 4
    for unit in (1, radix):
        digit = block // unit % radix
        turned = [None] * groups
        for i in range(groups):
            mine = i // unit % radix
            total = held[i]
            for other in range(radix):
                if other != mine:
                    moved = pltpu.roll(
                        held[i + (other - mine) * unit], (other - mine) * unit * WIDE % LANES, 1
                    )
                    total = jnp.where(digit == other, moved, total)
            turned[i] = total
        held = turned
    for i in range(groups):
        r, p, s = i // (POLS * SPECTRA), i // SPECTRA % POLS, i % SPECTRA
        out_ref[:, r, p, s, :] = held[i]


def total(parts):
    vmem = pl.BlockSpec(memory_space=pltpu.VMEM)
    return pl.pallas_call(
        sum_kernel,
        out_shape=jax.ShapeDtypeStruct((8, 2, POLS, SPECTRA, LANES), jnp.float32),
        in_specs=[vmem],
        out_specs=vmem,
        compiler_params=pltpu.CompilerParams(vmem_limit_bytes=20 * 2**20),
        name="sum_groups",
    )(parts)


def exchange(blocks, axis, first):
    order = leading(first, blocks.shape[0])
    return lax.all_to_all(
        blocks, axis, split_axis=0, concat_axis=0, axis_index_groups=[order], tiled=True
    )


def shards(voltages, beam_weights, owner_table, live_stations):
    spectra, weights, spread = channelize(voltages, owner_table, live_stations, beam_weights)
    turned = exchange(spectra, "chan", CHAN_LEAD)
    partial = beamform(turned, weights, spread)
    gathered = exchange(partial, "grp", GRP_LEAD)
    return total(gathered)


def solution(mesh):
    in_specs = (
        P(("grp", "chan"), None, None, None),
        P("grp", "chan", None, None),
        P(),
        P(("grp", "chan")),
    )
    out_specs = P("grp", None, None, None, "chan")
    return jax.shard_map(shards, mesh=mesh, in_specs=in_specs, out_specs=out_specs, check_vma=False)
```

```python
import functools

import jax
import jax.numpy as jnp
import numpy as np
from jax import lax
from jax.experimental import pallas as pl
from jax.experimental.pallas import tpu as pltpu
from jax.sharding import PartitionSpec as P

CHANNELS = 4096
TAPS = 16
BEAMS = 128
POLS = 2
SPECTRA = 4
FRAMES = SPECTRA + TAPS - 1
LANES = 128
FIRST = CHANNELS // LANES
ROWS = 2 * FIRST
PARTS = 2 * POLS * SPECTRA
HALF = FIRST // 2
WIDE = 8
CHAN_LEAD = 31
GRP_LEAD = 10


def leading(first, count):
    return [first] + [i for i in range(count) if i != first]


def tap_rows():
    total = TAPS * CHANNELS
    place = np.arange(total, dtype=np.float64)
    window = 0.54 - 0.46 * np.cos(2.0 * np.pi * place / total)
    taps = window * np.sinc((place - total // 2) / CHANNELS) / np.sqrt(CHANNELS)
    taps = taps.reshape(TAPS, FIRST, 1, LANES)
    return np.broadcast_to(taps, (TAPS, FIRST, 2, LANES)).reshape(TAPS, ROWS, LANES)


def first_matrix():
    k, q = np.arange(FIRST)[:, None], np.arange(FIRST)[None, :]
    angle = 2.0 * np.pi * (k * q % FIRST) / FIRST
    cosine, sine = np.cos(angle), np.sin(angle)
    real = np.stack([cosine, sine], 2).reshape(FIRST, ROWS)
    imag = np.stack([-sine, cosine], 2).reshape(FIRST, ROWS)
    whole = np.concatenate([real, imag], 0)
    high = whole.astype(jnp.bfloat16)
    low = (whole - high.astype(np.float64)).astype(jnp.bfloat16)
    return np.concatenate([high, low], 1)


def twiddles():
    k, n = np.arange(FIRST)[:, None], np.arange(LANES)[None, :]
    angle = 2.0 * np.pi * (k * n) / CHANNELS
    return np.stack([np.cos(angle), np.sin(angle)], 0).astype(np.float32)


def second_matrix():
    n, m = np.arange(LANES)[:, None], np.arange(LANES)[None, :]
    angle = 2.0 * np.pi * (n * m % LANES) / LANES
    cosine, sine = np.cos(angle), np.sin(angle)
    return np.block([[cosine, -sine], [sine, cosine]]).astype(jnp.bfloat16)


def spread_matrix(stations):
    out = np.zeros((POLS, 2, stations, POLS, stations, WIDE, 2), np.float32)
    for p in range(POLS):
        for i, st in enumerate(leading(CHAN_LEAD, stations)):
            out[p, 0, i, p, st, :, 0] = 1.0
            out[p, 1, i, p, st, :, 1] = -1.0
    return out.reshape(POLS * 2 * stations, POLS * stations * WIDE * 2).astype(jnp.bfloat16)


def channel_kernel(
    v_hbm,
    owner_hbm,
    live_ref,
    taps_hbm,
    matrix_hbm,
    w_hbm,
    spread_hbm,
    out_ref,
    w_ref,
    spread_ref,
    v_ref,
    owner_ref,
    taps_ref,
    matrix_ref,
    pick_ref,
    sem,
):
    f32, bf16 = jnp.float32, jnp.bfloat16
    pairs = [
        (owner_hbm, owner_ref),
        (taps_hbm, taps_ref),
        (v_hbm, v_ref),
        (matrix_hbm, matrix_ref),
        (spread_hbm, spread_ref),
        (w_hbm, w_ref),
    ]
    copies = [pltpu.make_async_copy(a, b, sem.at[i]) for i, (a, b) in enumerate(pairs)]
    for copy in copies:
        copy.start()
    blocks = out_ref.shape[0]
    count = POLS * SPECTRA

    copies[0].wait()
    rows = lax.broadcasted_iota(jnp.int32, (2 * LANES, LANES), 0).astype(f32).astype(bf16)
    one, zero = jnp.ones((), bf16), jnp.zeros((), bf16)
    for c in range(blocks):
        owner = owner_ref[c : c + 1, :]
        key = (((owner >> 4) & 1) * LANES + (owner >> 5)).astype(f32).astype(bf16)
        pick_ref[:, c * LANES : (c + 1) * LANES] = jnp.where(rows == key, one, zero)

    copies[1].wait()
    copies[2].wait()
    step = 16
    filtered = [[None] * (ROWS // step) for _ in range(count)]
    for p in range(POLS):
        for c in range(ROWS // step):
            sums = [None] * SPECTRA
            for u in range(FRAMES):
                x = v_ref[p, u * ROWS + c * step : u * ROWS + (c + 1) * step, :].astype(f32)
                for s in range(SPECTRA):
                    t = u - s
                    if 0 <= t < TAPS:
                        term = x * taps_ref[t, c * step : (c + 1) * step, :]
                        sums[s] = term if sums[s] is None else sums[s] + term
            for s in range(SPECTRA):
                filtered[p * SPECTRA + s][c] = sums[s].astype(bf16)
    columns = jnp.concatenate([jnp.concatenate(rows, 0) for rows in filtered], 1)
    copies[3].wait()
    first = jnp.dot(
        matrix_ref[:ROWS], jnp.concatenate([columns, columns], 0), preferred_element_type=f32
    )
    cosine, sine = taps_ref[TAPS, :FIRST], taps_ref[TAPS, FIRST:]
    halves = [[], []]
    for i in range(count):
        real = first[:FIRST, i * LANES : (i + 1) * LANES]
        imag = first[FIRST:, i * LANES : (i + 1) * LANES]
        halves[0].append(real * cosine + imag * sine)
        halves[1].append(imag * cosine - real * sine)
    folded = jnp.concatenate(
        [jnp.swapaxes(jnp.stack(h, 0), 0, 1).reshape(FIRST * count, LANES) for h in halves], 1
    ).astype(bf16)
    second = jnp.concatenate([matrix_ref[ROWS : 5 * LANES // 2], matrix_ref[5 * LANES // 2 :]], 1)
    spectrum = jnp.dot(folded, second, preferred_element_type=f32)
    spectrum = spectrum.astype(bf16).astype(f32) * live_ref[0].astype(f32)
    cut = HALF * count
    table = jnp.concatenate(
        [
            jnp.concatenate([spectrum[:cut, :LANES], spectrum[cut:, :LANES]], 1),
            jnp.concatenate([spectrum[:cut, LANES:], spectrum[cut:, LANES:]], 1),
        ],
        0,
    ).astype(bf16)
    place_of = {c: i for i, c in enumerate(leading(CHAN_LEAD, blocks))}
    for c in range(0, blocks, 2):
        found = jnp.dot(
            table, pick_ref[:, c * LANES : (c + 2) * LANES], preferred_element_type=f32
        )
        for d in range(2):
            low = jnp.broadcast_to(owner_ref[c + d : c + d + 1, :] & 15, (count, LANES))
            parts = []
            for r in range(2):
                block = found[r * cut : (r + 1) * cut, d * LANES : (d + 1) * LANES]
                total = block[:count]
                for h in range(1, HALF):
                    total = jnp.where(low == h, block[h * count : (h + 1) * count], total)
                parts.append(total)
            out_ref[place_of[c + d]] = jnp.concatenate(parts, 0).astype(bf16)
    copies[4].wait()
    copies[5].wait()


def place(array):
    return pltpu.with_memory_space_constraint(array, pltpu.HBM)


def channelize(volts, owner_table, live, weights):
    volts = volts.reshape(POLS, 2, FRAMES * FIRST, LANES)
    volts = jnp.transpose(volts, (0, 2, 1, 3)).reshape(POLS, FRAMES * ROWS, LANES)
    owner = owner_table.reshape(CHANNELS // LANES, LANES)
    stations = weights.shape[0]
    weights = weights.reshape(stations, LANES * 2, BEAMS)
    second = second_matrix()
    constants = [
        jnp.asarray(np.concatenate([tap_rows(), twiddles().reshape(1, ROWS, LANES)]), jnp.float32),
        jnp.asarray(np.concatenate([first_matrix(), second[:, :LANES], second[:, LANES:]])),
    ]
    spread = jnp.asarray(spread_matrix(stations))
    vmem = pl.BlockSpec(memory_space=pltpu.VMEM)
    hbm = pl.BlockSpec(memory_space=pltpu.HBM)
    held = [pltpu.VMEM(a.shape, a.dtype) for a in [volts, owner] + constants]
    return pl.pallas_call(
        channel_kernel,
        out_shape=[
            jax.ShapeDtypeStruct((CHANNELS // LANES, PARTS, LANES), jnp.bfloat16),
            jax.ShapeDtypeStruct(weights.shape, jnp.bfloat16),
            jax.ShapeDtypeStruct(spread.shape, jnp.bfloat16),
        ],
        in_specs=[hbm, hbm, pl.BlockSpec(memory_space=pltpu.SMEM)] + [hbm] * 4,
        out_specs=[vmem] * 3,
        scratch_shapes=held
        + [
            pltpu.VMEM((2 * LANES, CHANNELS), jnp.bfloat16),
            pltpu.SemaphoreType.DMA((6,)),
        ],
        compiler_params=pltpu.CompilerParams(vmem_limit_bytes=20 * 2**20),
        name="channelize",
    )(*[place(a) for a in (volts, owner)], live, *[place(a) for a in constants + [weights, spread]])


def beam_kernel(x_ref, w_ref, spread_ref, out_ref, wide_ref):
    f32, bf16 = jnp.float32, jnp.bfloat16
    stations = x_ref.shape[0]
    groups = LANES // WIDE
    wide_ref[...] = x_ref[...].reshape(stations * PARTS, LANES).astype(f32)
    turned = []
    for s in range(SPECTRA):
        rows = []
        for p in range(POLS):
            for r in range(2):
                start = r * POLS * SPECTRA + p * SPECTRA + s
                rows.append(wide_ref[pl.ds(start, stations, stride=PARTS), :])
        turned.append(jnp.concatenate(rows, 0).T)
    depth = stations * WIDE * 2
    height = SPECTRA * WIDE
    row_slot = lax.broadcasted_iota(jnp.int32, (height, depth), 0) % WIDE
    column_slot = lax.broadcasted_iota(jnp.int32, (height, depth), 1) // 2 % WIDE
    meets = row_slot == column_slot
    by_product = POLS
    small = []
    for g in range(groups):
        for s in range(SPECTRA):
            small.append(turned[s][g * WIDE : (g + 1) * WIDE])
    spread = jnp.dot(
        jnp.concatenate(small, 0).astype(bf16),
        spread_ref[...],
        preferred_element_type=f32,
    )
    lane = lax.broadcasted_iota(jnp.int32, (LANES, LANES), 1)
    held = LANES // (2 * WIDE)
    moved = {}
    for b in range(by_product, 2 * POLS):
        p = b % POLS
        for c in range(depth // LANES):
            station = c * held + lane // (2 * WIDE)
            at = jnp.where(station < CHAN_LEAD, station + 1, station)
            at = jnp.where(station == CHAN_LEAD, 0, at)
            index = (p * 2 + 1 - lane % 2) * stations + at
            for s in range(SPECTRA):
                moved[b, c, s] = jnp.take_along_axis(turned[s], index, axis=1)
    beams = []
    for g in range(groups):
        here = slice(g * WIDE, (g + 1) * WIDE)
        blocks = []
        for b in range(2 * POLS):
            if b < by_product:
                block = spread[g * height : (g + 1) * height, b * depth : (b + 1) * depth]
            else:
                block = jnp.concatenate(
                    [
                        jnp.concatenate([moved[b, c, s][here] for s in range(SPECTRA)], 0)
                        for c in range(depth // LANES)
                    ],
                    1,
                )
            blocks.append(jnp.where(meets, block, 0.0).astype(bf16))
        weights = w_ref[:, g * 2 * WIDE : (g + 1) * 2 * WIDE, :].reshape(depth, BEAMS)
        product = jnp.dot(jnp.concatenate(blocks, 0), weights, preferred_element_type=f32)
        beams.append(product.astype(bf16).T.astype(f32))
        if g % 2:
            where = g // 2 * 16
            for i, b in enumerate(leading(GRP_LEAD, out_ref.shape[0])):
                out_ref[i, where : where + 16, :] = jnp.concatenate(
                    [beams[g - 1 + d][8 * b : 8 * b + 8] for d in range(2)], 0
                ).astype(bf16)


def beamform(spectra, weights, spread):
    stations = weights.shape[0]
    groups = LANES // WIDE
    vmem = pl.BlockSpec(memory_space=pltpu.VMEM)
    return pl.pallas_call(
        beam_kernel,
        out_shape=jax.ShapeDtypeStruct((BEAMS // 8, 8 * groups, LANES), jnp.bfloat16),
        in_specs=[vmem] * 3,
        out_specs=vmem,
        scratch_shapes=[pltpu.VMEM((stations * PARTS, LANES), jnp.float32)],
        compiler_params=pltpu.CompilerParams(vmem_limit_bytes=20 * 2**20),
        name="beamform",
    )(spectra, weights, spread)


def sum_kernel(x_ref, out_ref):
    f32 = jnp.float32
    groups = LANES // WIDE
    held = []
    for g in range(0, groups, 2):
        total = x_ref[0, 8 * g : 8 * g + 16, :].astype(f32)
        for source in range(1, x_ref.shape[0]):
            total = total + x_ref[source, 8 * g : 8 * g + 16, :].astype(f32)
        held += [total[:8], total[8:]]
    block = lax.broadcasted_iota(jnp.int32, (8, LANES), 1) // WIDE
    radix = 4
    for unit in (1, radix):
        digit = block // unit % radix
        turned = [None] * groups
        for i in range(groups):
            mine = i // unit % radix
            total = held[i]
            for other in range(radix):
                if other != mine:
                    moved = pltpu.roll(
                        held[i + (other - mine) * unit], (other - mine) * unit * WIDE % LANES, 1
                    )
                    total = jnp.where(digit == other, moved, total)
            turned[i] = total
        held = turned
    for i in range(groups):
        r, p, s = i // (POLS * SPECTRA), i // SPECTRA % POLS, i % SPECTRA
        out_ref[:, r, p, s, :] = held[i]


def total(parts):
    vmem = pl.BlockSpec(memory_space=pltpu.VMEM)
    return pl.pallas_call(
        sum_kernel,
        out_shape=jax.ShapeDtypeStruct((8, 2, POLS, SPECTRA, LANES), jnp.float32),
        in_specs=[vmem],
        out_specs=vmem,
        compiler_params=pltpu.CompilerParams(vmem_limit_bytes=20 * 2**20),
        name="sum_groups",
    )(parts)


def exchange(blocks, axis, first):
    order = leading(first, blocks.shape[0])
    return lax.all_to_all(
        blocks, axis, split_axis=0, concat_axis=0, axis_index_groups=[order], tiled=True
    )


def shards(voltages, beam_weights, owner_table, live_stations):
    spectra, weights, spread = channelize(voltages, owner_table, live_stations, beam_weights)
    turned = exchange(spectra, "chan", CHAN_LEAD)
    partial = beamform(turned, weights, spread)
    gathered = exchange(partial, "grp", GRP_LEAD)
    return total(gathered)


def solution(mesh):
    in_specs = (
        P(("grp", "chan"), None, None, None),
        P("grp", "chan", None, None),
        P(),
        P(("grp", "chan")),
    )
    out_specs = P("grp", None, None, None, "chan")
    return jax.shard_map(shards, mesh=mesh, in_specs=in_specs, out_specs=out_specs, check_vma=False)
```
